256 devices in a mesh: tok: 32 (over x_lo, z, core), voc: 8 (over y, x_hi).
Axes of the slice: x: 4 (x_hi: 2, x_lo: 2; x = x_hi * 2 + x_lo), y: 4, z: 8, core: 2. Of those that a mesh axis runs over, the one named last changes fastest.
Arguments:
- hidden: bfloat16 [4096, 1792], P('tok'), may hold values from -40 to 40
- head_weight: bfloat16 [1792, 131072], P(None, ('voc', 'tok')), may hold values from -0.37796447 to 0.37796447
- teacher_probs: bfloat16 [4096, 131072], P('tok', 'voc'), may hold values from 0 to 1, as said below
- teacher_row: int32 [4096], replicated, may hold values from 0 to 4095, each once
- lengths: int32 [32], replicated, may hold values from 1 to 128, as said below
Outputs:
- head_grad: bfloat16 [1792, 131072], P(None, ('voc', 'tok'))
The draws below stay inside these ranges and needn't reach their ends.
Inputs may be any that keep to these rules, and one draw needn't show every extreme that they name: `teacher_row`: a permutation of the 4096 token positions. `lengths`: the last sequence is full. `teacher_probs`: each row is a probability distribution over the vocabulary: its entries sum to 1 up to rounding.
All inputs are finite; a program needn't handle non-finite values.
Results may differ from the reference program's by a relative error of at most 0.008.
Values may be sent and summed in bfloat16 or wider, within the bound.
No kernel may reach another device: no remote copies, remote signals or barrier semaphores. Data moves between devices by JAX's collectives and lax.ppermute only.
A program may use at most 128 MiB of HBM per device.

```python
import jax
import jax.numpy as jnp
from jax import lax

D = 1792
VOC_SUB = 512
SEQ_LEN = 128
TOKENS = 4096
VOCAB = 131072
SEQS = 32


def draw_hidden(key, part):
    key = jax.random.fold_in(key, 1)
    key_rows, key_base = jax.random.split(key, 2)
    row_scale = jnp.exp(jax.random.uniform(key_rows, (TOKENS, 1), jnp.float32, 0.0, jnp.log(10.0)))
    base = jax.random.truncated_normal(key_base, -4.0, 4.0, (TOKENS, D), jnp.float32) * row_scale
    return base.astype(jnp.bfloat16)


def draw_head_weight(key, part):
    key = jax.random.fold_in(key, 2)
    key_cols, key_base = jax.random.split(key)
    col_scale = jnp.exp(jax.random.uniform(key_cols, (VOCAB,), jnp.float32, jnp.log(0.4), jnp.log(4.0)))
    weight = jax.random.truncated_normal(key_base, -4.0, 4.0, (D, VOCAB), jnp.float32) * col_scale[None, :] / jnp.sqrt(jnp.float32(D))
    return weight.astype(jnp.bfloat16)


def draw_teacher_probs(key, part):
    key = jax.random.fold_in(key, 4)
    key_rows, key_vals = jax.random.split(key)
    row_scale = jnp.exp(jax.random.uniform(key_rows, (TOKENS, 1), jnp.float32, jnp.log(2.5), jnp.log(5.0)))
    values = jax.random.truncated_normal(key_vals, -4.5, 4.5, (TOKENS, VOCAB), jnp.float32)
    teacher_logits = values * row_scale
    return jax.nn.softmax(teacher_logits, axis=1).astype(jnp.bfloat16)


def draw_lengths(key, part):
    key = jax.random.fold_in(key, 13)
    index = jnp.arange(SEQS, dtype=jnp.int32)
    lowest = SEQ_LEN // 8 + SEQ_LEN // 2 * index // SEQS
    extra = jax.random.randint(key, (SEQS,), 0, SEQ_LEN // 2 + 1, jnp.int32)
    drawn = jnp.clip(lowest + extra, 1, SEQ_LEN)
    return jnp.where(index == SEQS - 1, SEQ_LEN, drawn).astype(jnp.int32)


def setup_inputs(seed: int = 0) -> dict:
    arg_keys = jax.random.split(jax.random.key(seed), 6)
    hidden = draw_hidden(jax.random.fold_in(arg_keys[5], 71), 0)
    head_weight = draw_head_weight(jax.random.fold_in(arg_keys[5], 71), 0)
    teacher_probs = draw_teacher_probs(jax.random.fold_in(arg_keys[5], 71), 0)
    teacher_row = jax.random.permutation(arg_keys[3], TOKENS).astype(jnp.int32)
    lengths = draw_lengths(jax.random.fold_in(arg_keys[5], 71), 0)
    return {"hidden": hidden, "head_weight": head_weight, "teacher_probs": teacher_probs, "teacher_row": teacher_row, "lengths": lengths}


loss_scale = 1048576.0


def reference(hidden, head_weight, teacher_probs, teacher_row, lengths):
    blocks = VOCAB // VOC_SUB
    weight_blocks = head_weight.reshape(D, blocks, VOC_SUB).transpose(1, 0, 2)
    teacher_blocks = teacher_probs.reshape(TOKENS, blocks, VOC_SUB).transpose(1, 0, 2)

    def stat_step(running, weight_block):
        old_peak, old_total = running
        logits = jnp.dot(hidden, weight_block, preferred_element_type=jnp.float32)
        new_peak = jnp.maximum(old_peak, jnp.max(logits, axis=1))
        new_total = old_total * jnp.exp(old_peak - new_peak) + jnp.sum(jnp.exp(logits - new_peak[:, None]), axis=1)
        return (new_peak, new_total), logits

    start_peak = jnp.full((TOKENS,), -jnp.inf, jnp.float32)
    start_total = jnp.zeros((TOKENS,), jnp.float32)
    (row_peak, row_total), stored = lax.scan(stat_step, (start_peak, start_total), weight_blocks)

    def pieces(logits, teacher_block):
        log_student = (logits - row_peak[:, None]) - jnp.log(row_total)[:, None]
        student = jnp.exp(log_student)
        aligned = jnp.take(teacher_block, teacher_row, axis=0).astype(jnp.float32)
        log_mix = jnp.log(0.5 * aligned + 0.5 * student)
        grad_prob = 0.5 * (log_student - log_mix)
        return student, grad_prob

    def centre_step(running, pair):
        student, grad_prob = pieces(pair[0], pair[1])
        return running + jnp.sum(student * grad_prob, axis=1), None

    centre, unused = lax.scan(centre_step, jnp.zeros((TOKENS,), jnp.float32), (stored, teacher_blocks))
    positions = jnp.arange(TOKENS, dtype=jnp.int32)
    limits = jnp.repeat(lengths, SEQ_LEN, total_repeat_length=TOKENS)
    valid_mask = (positions % SEQ_LEN < limits).astype(jnp.float32)
    token_count = jnp.sum(lengths).astype(jnp.float32)
    grad_scale = loss_scale / token_count

    def grad_block(pair):
        student, grad_prob = pieces(pair[0], pair[1])
        dlogits = (((grad_scale * valid_mask)[:, None] * student) * (grad_prob - centre[:, None])).astype(jnp.bfloat16)
        block_grad = lax.dot_general(hidden, dlogits, (((0,), (0,)), ((), ())), preferred_element_type=jnp.float32)
        return block_grad.astype(jnp.bfloat16)

    grads = lax.map(grad_block, (stored, teacher_blocks))
    return grads.transpose(1, 0, 2).reshape(D, VOCAB)
```

```python
import jax
import jax.numpy as jnp
from jax import lax
from jax.sharding import PartitionSpec as P

SEQ_LEN = 128


loss_scale = 1048576.0


def share_blocks(parts, tok, voc):
    k, rows = parts.shape
    blocks = parts.reshape(k, tok, rows // tok).transpose(1, 0, 2)
    return lax.all_to_all(blocks, "tok", split_axis=0, concat_axis=0, tiled=True)


def spread_blocks(block, tok, voc):
    k, part = block.shape
    copies = jnp.broadcast_to(block[None], (tok * voc, k, part))
    got = lax.all_to_all(copies, ("tok", "voc"), split_axis=0, concat_axis=0, tiled=True)
    return got.reshape(tok, voc, k, part).transpose(1, 2, 0, 3).reshape(voc, k, tok * part)


def merge_totals(peaks, totals):
    peak = jnp.max(peaks, axis=0)
    return peak, jnp.sum(totals * jnp.exp(peaks - peak[None]), axis=0)


def make_per_device(tok, voc):
    def per_device(hidden, head_weight, teacher_probs, teacher_row, lengths):
        gathered = lax.all_gather(hidden, "tok", axis=0, tiled=True)
        logits = jnp.dot(gathered, head_weight, preferred_element_type=jnp.float32)
        teacher = lax.all_to_all(teacher_probs, "tok", split_axis=1, concat_axis=0, tiled=True)
        aligned = jnp.take(teacher, teacher_row, axis=0).astype(jnp.float32)
        local_peak = jnp.max(logits, axis=1)
        local_total = jnp.sum(jnp.exp(logits - local_peak[:, None]), axis=1)
        terms = share_blocks(jnp.stack([local_peak, local_total]), tok, voc)
        terms = spread_blocks(jnp.stack(merge_totals(terms[:, 0], terms[:, 1])), tok, voc)
        row_peak, row_total = merge_totals(terms[:, 0], terms[:, 1])
        log_student = logits - row_peak[:, None] - jnp.log(row_total)[:, None]
        student = jnp.exp(log_student)
        log_mix = jnp.log(0.5 * aligned + 0.5 * student)
        grad_prob = 0.5 * (log_student - log_mix)
        local_centre = jnp.sum(student * grad_prob, axis=1)
        terms = share_blocks(local_centre[None], tok, voc)
        centre = jnp.sum(spread_blocks(jnp.sum(terms, axis=0), tok, voc), axis=0)[0]
        rows_all = logits.shape[0]
        positions = jnp.arange(rows_all, dtype=jnp.int32)
        limits = jnp.repeat(lengths, SEQ_LEN, total_repeat_length=rows_all)
        valid_mask = (positions % SEQ_LEN < limits).astype(jnp.float32)
        token_count = jnp.sum(lengths).astype(jnp.float32)
        grad_scale = loss_scale / token_count
        dlogits = ((grad_scale * valid_mask)[:, None] * student * (grad_prob - centre[:, None])).astype(
            jnp.bfloat16
        )
        head_grad = lax.dot_general(
            gathered, dlogits, (((0,), (0,)), ((), ())), preferred_element_type=jnp.float32
        )
        return head_grad.astype(jnp.bfloat16)

    return per_device


def solution(mesh):
    return jax.shard_map(
        make_per_device(mesh.shape["tok"], mesh.shape["voc"]),
        mesh=mesh,
        in_specs=(P("tok", None), P(None, ("voc", "tok")), P("tok", "voc"), P(), P()),
        out_specs=P(None, ("voc", "tok")),
        check_vma=False,
    )
```

```python
import functools

import jax
import jax.numpy as jnp
from jax import lax
from jax.experimental import pallas as pl
from jax.experimental.pallas import tpu as pltpu
from jax.sharding import PartitionSpec as P

SEQ_LEN = 128
AXES = ("tok", "voc")

NX, NY, NZ = 4, 4, 8


loss_scale = 1048576.0


def linear(x, y, z, core):
    x, y, z = x % NX, y % NY, z % NZ
    return (((x % 2) * NZ + z) * 2 + core) * (NY * 2) + y * 2 + x // 2


def hop(array, dx=0, dy=0, dz=0, flip=0):
    pairs = [
        (linear(x, y, z, core), linear(x + dx, y + dy, z + dz, core ^ flip))
        for x in range(NX)
        for y in range(NY)
        for z in range(NZ)
        for core in range(2)
    ]
    return lax.ppermute(array, AXES, pairs)


TURNS = (0, -1, 1, 2)


def spread_over_z(hidden):
    rows = hidden.shape[0] // NY
    y = lax.axis_index("voc") // 2
    own = lax.dynamic_slice_in_dim(hidden, y * rows, rows, 0)
    up, down = [own], [own]
    for step in range(1, 4):
        up.append(hop(up[-1], dz=1))
        down.append(hop(down[-1], dz=-1))
    up.append(hop(up[-1], dz=1))
    return jnp.stack([up[0], up[1], up[2], up[3]]), jnp.stack([up[4], down[3], down[2], down[1]])


def spread_over_plane(half_a, half_b):
    prev_a, prev_b = hop(half_a, dy=1), hop(half_b, dy=1)
    next_a, next_b = hop(half_a, dy=-1), hop(half_b, dy=-1)
    far_a, far_b = hop(prev_a, dy=1), hop(next_b, dy=-1)
    held = {}
    for half, arrays in enumerate(((half_a, prev_a, next_a, far_a), (half_b, prev_b, next_b, far_b))):
        for turn, array in zip(TURNS, arrays):
            crossed = hop(array, dx=1 if half == 0 else -1)
            for other, piece in enumerate((array, crossed)):
                held[half, other, turn, 0] = piece
                held[half, other, turn, 1] = hop(piece, flip=1)
    return held


def coords():
    tok, voc = lax.axis_index("tok"), lax.axis_index("voc")
    return jnp.stack([tok // (2 * NZ), lax.rem(tok // 2, NZ), lax.rem(tok, 2), voc // 2]).astype(jnp.int32)


def logits_kernel(keys, place, *refs):
    pieces, (weight, hidden, logits, peak, total) = refs[: len(keys)], refs[len(keys) :]
    rows = pieces[0].shape[1]
    column, k = pl.program_id(0), pl.program_id(1)
    for half in range(2):
        for other in range(2):

            @pl.when((column == other) & (k // 4 == half))
            def _():
                for (piece_half, piece_other, turn, flip), piece in zip(keys, pieces):
                    if (piece_half, piece_other) == (half, other):
                        core = 1 - place[2] if flip else place[2]
                        start = core * (rows * NY) + lax.rem(place[3] + turn + NY, NY) * rows
                        hidden[pl.ds(pl.multiple_of(start, rows), rows), :] = piece[0]

    values = jnp.dot(hidden[...], weight[...], preferred_element_type=jnp.float32)
    logits[...] = values
    row_peak = jnp.max(values, axis=1, keepdims=True)
    row_total = jnp.sum(jnp.exp(values - row_peak), axis=1, keepdims=True)
    wide = (values.shape[0], 128)
    peak[0] = jnp.broadcast_to(row_peak, wide).T[:1]
    total[0] = jnp.broadcast_to(row_total, wide).T[:1]


def block_logits(held, weight):
    keys = tuple(sorted(held))
    pieces = [held[key] for key in keys]
    rows, depth = pieces[0].shape[1:]
    width = weight.shape[1]
    block = 2 * NY * rows
    blocks = 2 * NZ

    def piece_index(half, other):
        def index(column, k, place):
            inner = jnp.clip(k - 4 * half, 0, 3)
            return (jnp.where(column == other, inner, 3 if other == 0 else 0), 0, 0)

        return index

    def token_block(column, k, place):
        x_lo = jnp.where(column == 0, place[0], 1 - place[0])
        return x_lo * NZ + lax.rem(place[1] + NZ - k, NZ)

    out = pl.pallas_call(
        functools.partial(logits_kernel, keys),
        grid_spec=pltpu.PrefetchScalarGridSpec(
            num_scalar_prefetch=1,
            grid=(2, NZ),
            in_specs=[pl.BlockSpec((1, rows, depth), piece_index(key[0], key[1])) for key in keys]
            + [pl.BlockSpec((depth, width), lambda *_: (0, 0))],
            out_specs=[
                pl.BlockSpec((block, depth), lambda *args: (token_block(*args), 0)),
                pl.BlockSpec((block, width), lambda *args: (token_block(*args), 0)),
                pl.BlockSpec((1, 1, block), lambda *args: (token_block(*args), 0, 0)),
                pl.BlockSpec((1, 1, block), lambda *args: (token_block(*args), 0, 0)),
            ],
        ),
        out_shape=[
            jax.ShapeDtypeStruct((blocks * block, depth), jnp.bfloat16),
            jax.ShapeDtypeStruct((blocks * block, width), jnp.float32),
            jax.ShapeDtypeStruct((blocks, 1, block), jnp.float32),
            jax.ShapeDtypeStruct((blocks, 1, block), jnp.float32),
        ],
        compiler_params=pltpu.CompilerParams(vmem_limit_bytes=40 * 1024 * 1024),
        cost_estimate=pl.CostEstimate(
            flops=2 * blocks * block * depth * width,
            transcendentals=blocks * block * width,
            bytes_accessed=blocks * block * (4 * depth + 4 * width) + 2 * depth * width,
        ),
    )(coords(), *pieces, weight)
    tokens, scores, peak, total = out
    return tokens, scores, peak.reshape(-1), total.reshape(-1)


def share_blocks(parts, tok, voc):
    k, rows = parts.shape
    blocks = parts.reshape(k, tok, rows // tok).transpose(1, 0, 2)
    return lax.all_to_all(blocks, "tok", split_axis=0, concat_axis=0, tiled=True)


def spread_blocks(block, tok, voc):
    k, part = block.shape
    copies = jnp.broadcast_to(block[None], (tok * voc, k, part))
    got = lax.all_to_all(copies, ("tok", "voc"), split_axis=0, concat_axis=0, tiled=True)
    return got.reshape(tok, voc, k, part).transpose(1, 2, 0, 3).reshape(voc, k, tok * part)


def merge_totals(peaks, totals):
    peak = jnp.max(peaks, axis=0)
    return peak, jnp.sum(totals * jnp.exp(peaks - peak[None]), axis=0)


def make_per_device(tok, voc):
    def per_device(hidden, head_weight, teacher_probs, teacher_row, lengths):
        rows_all = hidden.shape[0] * tok
        half_a, half_b = spread_over_z(hidden)
        half_a, half_b, teacher_probs = lax.optimization_barrier((half_a, half_b, teacher_probs))
        teacher = lax.all_to_all(teacher_probs, "tok", split_axis=1, concat_axis=0, tiled=True)
        aligned = jnp.take(teacher, teacher_row, axis=0).astype(jnp.float32)
        held = spread_over_plane(half_a, half_b)
        gathered, logits, local_peak, local_total = block_logits(held, head_weight)
        terms = share_blocks(jnp.stack([local_peak, local_total]), tok, voc)
        terms = spread_blocks(jnp.stack(merge_totals(terms[:, 0], terms[:, 1])), tok, voc)
        row_peak, row_total = merge_totals(terms[:, 0], terms[:, 1])
        log_student = logits - row_peak[:, None] - jnp.log(row_total)[:, None]
        student = jnp.exp(log_student)
        log_mix = jnp.log(0.5 * aligned + 0.5 * student)
        grad_prob = 0.5 * (log_student - log_mix)
        local_centre = jnp.sum(student * grad_prob, axis=1)
        terms = share_blocks(local_centre[None], tok, voc)
        centre = jnp.sum(spread_blocks(jnp.sum(terms, axis=0), tok, voc), axis=0)[0]
        positions = jnp.arange(rows_all, dtype=jnp.int32)
        limits = jnp.repeat(lengths, SEQ_LEN, total_repeat_length=rows_all)
        valid_mask = (positions % SEQ_LEN < limits).astype(jnp.float32)
        token_count = jnp.sum(lengths).astype(jnp.float32)
        grad_scale = loss_scale / token_count
        dlogits = ((grad_scale * valid_mask)[:, None] * student * (grad_prob - centre[:, None])).astype(
            jnp.bfloat16
        )
        head_grad = lax.dot_general(
            gathered, dlogits, (((0,), (0,)), ((), ())), preferred_element_type=jnp.float32
        )
        return head_grad.astype(jnp.bfloat16)

    return per_device


def solution(mesh):
    return jax.shard_map(
        make_per_device(mesh.shape["tok"], mesh.shape["voc"]),
        mesh=mesh,
        in_specs=(P("tok", None), P(None, ("voc", "tok")), P("tok", "voc"), P(), P()),
        out_specs=P(None, ("voc", "tok")),
        check_vma=False,
    )
```

```python
import functools

import jax
import jax.numpy as jnp
from jax import lax
from jax.experimental import pallas as pl
from jax.experimental.pallas import tpu as pltpu
from jax.sharding import PartitionSpec as P

SEQ_LEN = 128
AXES = ("tok", "voc")

NX, NY, NZ = 4, 4, 8


loss_scale = 1048576.0


def linear(x, y, z, core):
    x, y, z = x % NX, y % NY, z % NZ
    return (((x % 2) * NZ + z) * 2 + core) * (NY * 2) + y * 2 + x // 2


def hop(array, dx=0, dy=0, dz=0, flip=0):
    pairs = [
        (linear(x, y, z, core), linear(x + dx, y + dy, z + dz, core ^ flip))
        for x in range(NX)
        for y in range(NY)
        for z in range(NZ)
        for core in range(2)
    ]
    return lax.ppermute(array, AXES, pairs)


TURNS = (0, -1, 1, 2)


def spread_over_z(hidden):
    rows = hidden.shape[0] // NY
    y = lax.axis_index("voc") // 2
    own = lax.dynamic_slice_in_dim(hidden, y * rows, rows, 0)
    up, down = [own], [own]
    for step in range(1, 4):
        up.append(hop(up[-1], dz=1))
        down.append(hop(down[-1], dz=-1))
    up.append(hop(up[-1], dz=1))
    return jnp.stack([up[0], up[1], up[2], up[3]]), jnp.stack([up[4], down[3], down[2], down[1]])


def cross(array, near):
    pairs = [
        (linear(x, y, z, core), linear(x + 1 if (x % 2 == 0) == near else x - 1, y, z, core))
        for x in range(NX)
        for y in range(NY)
        for z in range(NZ)
        for core in range(2)
    ]
    return lax.ppermute(array, AXES, pairs)


def tie(*groups):
    return lax.optimization_barrier(groups)


def flip_core(arrays):
    return [hop(array, flip=1) for array in arrays]


def gather_logits(place, half_a, half_b, weight):
    own, crossed, own_flip, crossed_flip = {}, {}, {}, {}
    prev_a, next_b = hop(half_a, dy=1), hop(half_b, dy=-1)
    prev_b, next_a = hop(half_b, dy=1), hop(half_a, dy=-1)
    cross_a, cross_b = cross(half_a, near=True), cross(half_b, near=False)
    prev_a, next_b, cross_a, cross_b = tie(prev_a, next_b, cross_a, cross_b)
    far_a, far_b = hop(prev_a, dy=1), hop(next_b, dy=-1)
    firsts = half_a, half_b, cross_a, cross_b
    seconds = prev_a, prev_b, next_a, next_b
    firsts_flip = flip_core(firsts)
    seconds_cross = [cross(array, near=near) for array, near in zip(seconds, (True, False, False, False))]
    seconds, seconds_cross, far_a, far_b, firsts_flip = tie(seconds, seconds_cross, far_a, far_b, firsts_flip)
    far_cross = cross(far_a, near=True), cross(far_b, near=False)
    seconds_flip = flip_core(seconds)
    far_flip = flip_core((far_a, far_b))
    own = {
        (0, 0, 0, 0): firsts[0], (1, 0, 0, 0): firsts[1], (0, 0, 0, 1): firsts_flip[0], (1, 0, 0, 1): firsts_flip[1],
        (0, 0, 2, 0): far_a, (1, 0, 2, 0): far_b, (0, 0, 2, 1): far_flip[0], (1, 0, 2, 1): far_flip[1],
    }
    crossed = {
        (0, 1, 0, 0): firsts[2], (1, 1, 0, 0): firsts[3], (0, 1, 0, 1): firsts_flip[2], (1, 1, 0, 1): firsts_flip[3],
    }
    seconds_cross_flip = flip_core(seconds_cross)
    for i, (half, turn) in enumerate(((0, -1), (1, -1), (0, 1), (1, 1))):
        own[half, 0, turn, 0], own[half, 0, turn, 1] = seconds[i], seconds_flip[i]
        crossed[half, 1, turn, 0], crossed[half, 1, turn, 1] = seconds_cross[i], seconds_cross_flip[i]
    done = block_logits(place, own, weight, 0, None)
    done, far_cross = tie(done, far_cross)
    for half, (array, other) in enumerate(zip(far_cross, flip_core(far_cross))):
        crossed[half, 1, 2, 0], crossed[half, 1, 2, 1] = array, other
    return block_logits(place, crossed, weight, 1, done)


def coords():
    tok, voc = lax.axis_index("tok"), lax.axis_index("voc")
    return jnp.stack([tok // (2 * NZ), lax.rem(tok // 2, NZ), lax.rem(tok, 2), voc // 2]).astype(jnp.int32)


def token_block(place, column, k):
    x_lo = jnp.where(column == 0, place[0], 1 - place[0])
    return x_lo * NZ + lax.rem(place[1] + NZ - k, NZ)


def to_local(values, place):
    order = jnp.stack([token_block(place, column, k) for column in range(2) for k in range(NZ)])
    return values.reshape(2 * NZ, -1)[order].reshape(-1)


def from_local(values, place):
    order = jnp.stack([token_block(place, x_lo, z) for x_lo in range(2) for z in range(NZ)])
    return values.reshape(2 * NZ, -1)[order].reshape(-1)


def logits_kernel(keys, column, place, *refs):
    pieces = refs[: len(keys)]
    weight, peak_before, total_before = refs[len(keys) : len(keys) + 3]
    hidden, logits, peak, total, slots, load_sem, store_sem = refs[-7:]
    rows = pieces[0].shape[1]
    step, steps = pl.program_id(0), pl.num_programs(0)

    @pl.when(step == 0)
    def _():
        for group in range(2):
            for (half, _, turn, flip), piece in zip(keys, pieces):
                if half == group:
                    core = 1 - place[2] if flip else place[2]
                    start = core * (rows * NY) + lax.rem(place[3] + turn + NY, NY) * rows
                    to = slots.at[group, :, pl.ds(pl.multiple_of(start, rows), rows)]
                    pltpu.make_async_copy(piece, to, load_sem.at[group]).start()
        peak[...] = peak_before[...]
        total[...] = total_before[...]

    def store(group):
        return pltpu.make_async_copy(slots.at[group], hidden.at[2 * column + group], store_sem.at[group])

    pltpu.make_async_copy(slots.at[step], slots.at[step], load_sem.at[step]).wait()
    store(step).start()
    tokens = slots[step].reshape(logits.shape[0], slots.shape[-1])
    values = jnp.dot(tokens, weight[...], preferred_element_type=jnp.float32)
    logits[...] = values
    row_peak = jnp.max(values, axis=1, keepdims=True)
    row_total = jnp.sum(jnp.exp(values - row_peak), axis=1, keepdims=True)
    wide = (values.shape[0], 128)
    for out, stat in ((peak, row_peak), (total, row_total)):
        line = jnp.broadcast_to(stat, wide).T[:1]
        width = out.shape[-1]
        for part in range(4):
            out[token_block(place, column, step * 4 + part)] = line[:, part * width : (part + 1) * width]

    @pl.when(step + 1 == steps)
    def _():
        for group in range(2):
            store(group).wait()


def block_logits(place, held, weight, column, before):
    keys = tuple(sorted(key for key in held if key[1] == column))
    pieces = [held[key] for key in keys]
    rows, depth = pieces[0].shape[1:]
    width = weight.shape[1]
    block = 2 * NY * rows
    blocks = 2 * NZ
    stat = jax.ShapeDtypeStruct((blocks, 1, block), jnp.float32)
    stat_spec = pl.BlockSpec((blocks, 1, block), lambda step, place: (0, 0, 0))
    any_spec = pl.BlockSpec(memory_space=pl.ANY)
    if before is None:
        extra = [jnp.zeros(stat.shape, stat.dtype)] * 2
        aliases = {}
    else:
        extra = [before[2], before[3], before[0], before[1]]
        aliases = {len(keys) + 4: 0, len(keys) + 5: 1}
    return pl.pallas_call(
        functools.partial(logits_kernel, keys, column),
        grid_spec=pltpu.PrefetchScalarGridSpec(
            num_scalar_prefetch=1,
            grid=(2,),
            in_specs=[any_spec] * len(keys)
            + [pl.BlockSpec((depth, width), lambda *_: (0, 0)), stat_spec, stat_spec]
            + [any_spec] * (len(extra) - 2),
            out_specs=[
                any_spec,
                pl.BlockSpec((4 * block, width), lambda step, place: (2 * column + step, 0)),
                stat_spec,
                stat_spec,
            ],
            scratch_shapes=[
                pltpu.VMEM((2, 4, block, depth), jnp.bfloat16),
                pltpu.SemaphoreType.DMA((2,)),
                pltpu.SemaphoreType.DMA((2,)),
            ],
        ),
        out_shape=[
            jax.ShapeDtypeStruct((4, 4, block, depth), jnp.bfloat16),
            jax.ShapeDtypeStruct((blocks * block, width), jnp.float32),
            stat,
            stat,
        ],
        input_output_aliases=aliases,
        compiler_params=pltpu.CompilerParams(vmem_limit_bytes=56 * 1024 * 1024),
        cost_estimate=pl.CostEstimate(
            flops=blocks * block * depth * width,
            transcendentals=blocks * block * width // 2,
            bytes_accessed=blocks * block * (2 * depth + 2 * width) + 2 * depth * width,
        ),
    )(place, *pieces, weight, *extra)


def rows_kernel(chosen, teacher, aligned, narrow, wide, sem):
    step = pl.program_id(0)
    count = aligned.shape[0]
    parts = sem.shape[0]
    part = narrow.shape[0] // parts

    @pl.when(step == 0)
    def _():
        def load(i):
            span = pl.ds(i * part, part)
            return pltpu.make_async_copy(teacher.at[span], narrow.at[span], sem.at[i])

        for i in range(parts):
            load(i).start()
        for i in range(parts):
            load(i).wait()
            wide[pl.ds(i * part, part), :] = narrow[pl.ds(i * part, part), :].astype(jnp.float32)

    @pl.loop(0, count // 16, unroll=4)
    def _(group):
        first = step * count + group * 16
        picked = [wide[pl.ds(chosen[first + i], 1), :] for i in range(16)]
        rows = jnp.concatenate(picked, axis=0).astype(jnp.bfloat16)
        aligned[pl.ds(pl.multiple_of(group * 16, 16), 16), :] = rows


def take_rows(teacher, chosen):
    rows, width = teacher.shape
    count = rows // 4
    return pl.pallas_call(
        rows_kernel,
        grid_spec=pltpu.PrefetchScalarGridSpec(
            num_scalar_prefetch=1,
            grid=(4,),
            in_specs=[pl.BlockSpec(memory_space=pl.ANY)],
            out_specs=pl.BlockSpec((count, width), lambda step, chosen: (step, 0)),
            scratch_shapes=[
                pltpu.VMEM((rows, width), jnp.bfloat16),
                pltpu.VMEM((rows, width), jnp.float32),
                pltpu.SemaphoreType.DMA((8,)),
            ],
        ),
        out_shape=jax.ShapeDtypeStruct((rows, width), jnp.bfloat16),
        compiler_params=pltpu.CompilerParams(vmem_limit_bytes=56 * 1024 * 1024),
        cost_estimate=pl.CostEstimate(flops=0, transcendentals=0, bytes_accessed=10 * rows * width * 2),
    )(chosen, teacher)


def share_blocks(parts, tok, voc):
    k, rows = parts.shape
    blocks = parts.reshape(k, tok, rows // tok).transpose(1, 0, 2)
    return lax.all_to_all(blocks, "tok", split_axis=0, concat_axis=0, tiled=True)


def spread_blocks(block, tok, voc):
    k, part = block.shape
    copies = jnp.broadcast_to(block[None], (tok * voc, k, part))
    got = lax.all_to_all(copies, ("tok", "voc"), split_axis=0, concat_axis=0, tiled=True)
    return got.reshape(tok, voc, k, part).transpose(1, 2, 0, 3).reshape(voc, k, tok * part)


def merge_totals(peaks, totals):
    peak = jnp.max(peaks, axis=0)
    return peak, jnp.sum(totals * jnp.exp(peaks - peak[None]), axis=0)


def make_per_device(tok, voc):
    def per_device(hidden, head_weight, teacher_probs, teacher_row, lengths):
        rows_all = hidden.shape[0] * tok
        half_a, half_b = spread_over_z(hidden)
        by_owner = teacher_probs.reshape(teacher_probs.shape[0], tok, -1).transpose(1, 0, 2)
        half_a, half_b, by_owner = lax.optimization_barrier((half_a, half_b, by_owner))
        teacher = lax.all_to_all(by_owner, "tok", split_axis=0, concat_axis=0, tiled=True)
        place = coords()
        gathered, logits, local_peak, local_total = gather_logits(place, half_a, half_b, head_weight)
        gathered = gathered.reshape(rows_all, -1)
        local_peak, local_total, teacher = lax.optimization_barrier((local_peak, local_total, teacher))
        aligned = take_rows(teacher.reshape(rows_all, -1), to_local(teacher_row, place)).astype(jnp.float32)
        terms = share_blocks(jnp.stack([local_peak.reshape(-1), local_total.reshape(-1)]), tok, voc)
        terms = spread_blocks(jnp.stack(merge_totals(terms[:, 0], terms[:, 1])), tok, voc)
        row_peak, row_total = merge_totals(terms[:, 0], terms[:, 1])
        row_peak, row_total = to_local(row_peak, place), to_local(row_total, place)
        log_student = logits - row_peak[:, None] - jnp.log(row_total)[:, None]
        student = jnp.exp(log_student)
        log_mix = jnp.log(0.5 * aligned + 0.5 * student)
        grad_prob = 0.5 * (log_student - log_mix)
        local_centre = jnp.sum(student * grad_prob, axis=1)
        terms = share_blocks(from_local(local_centre, place)[None], tok, voc)
        centre = jnp.sum(spread_blocks(jnp.sum(terms, axis=0), tok, voc), axis=0)[0]
        centre = to_local(centre, place)
        positions = jnp.arange(SEQ_LEN, dtype=jnp.int32)
        valid_mask = (positions[None, :] < lengths[:, None]).astype(jnp.float32).reshape(-1)
        valid_mask = to_local(valid_mask, place)
        token_count = jnp.sum(lengths).astype(jnp.float32)
        grad_scale = loss_scale / token_count
        dlogits = ((grad_scale * valid_mask)[:, None] * student * (grad_prob - centre[:, None])).astype(
            jnp.bfloat16
        )
        head_grad = lax.dot_general(
            gathered, dlogits, (((0,), (0,)), ((), ())), preferred_element_type=jnp.float32
        )
        return head_grad.astype(jnp.bfloat16)

    return per_device


def solution(mesh):
    return jax.shard_map(
        make_per_device(mesh.shape["tok"], mesh.shape["voc"]),
        mesh=mesh,
        in_specs=(P("tok", None), P(None, ("voc", "tok")), P("tok", "voc"), P(), P()),
        out_specs=P(None, ("voc", "tok")),
        check_vma=False,
    )
```

```python
import functools

import jax
import jax.numpy as jnp
from jax import lax
from jax.experimental import pallas as pl
from jax.experimental.pallas import tpu as pltpu
from jax.sharding import PartitionSpec as P

SEQ_LEN = 128
AXES = ("tok", "voc")

NX, NY, NZ = 4, 4, 8


loss_scale = 1048576.0


def linear(x, y, z, core):
    x, y, z = x % NX, y % NY, z % NZ
    return (((x % 2) * NZ + z) * 2 + core) * (NY * 2) + y * 2 + x // 2


def hop(array, dx=0, dy=0, dz=0, flip=0):
    pairs = [
        (linear(x, y, z, core), linear(x + dx, y + dy, z + dz, core ^ flip))
        for x in range(NX)
        for y in range(NY)
        for z in range(NZ)
        for core in range(2)
    ]
    return lax.ppermute(array, AXES, pairs)


def spread_over_z(hidden):
    rows = hidden.shape[0] // NY
    y = lax.axis_index("voc") // 2
    own = lax.dynamic_slice_in_dim(hidden, y * rows, rows, 0)
    up, down = [own], [own]
    for step in range(1, 4):
        up.append(hop(up[-1], dz=1))
        down.append(hop(down[-1], dz=-1))
    up.append(hop(up[-1], dz=1))
    return jnp.stack([*up, down[3], down[2], down[1]])


def cross(array, near):
    pairs = [
        (linear(x, y, z, core), linear(x + 1 if (x % 2 == 0) == near else x - 1, y, z, core))
        for x in range(NX)
        for y in range(NY)
        for z in range(NZ)
        for core in range(2)
    ]
    return lax.ppermute(array, AXES, pairs)


def tie(*groups):
    return lax.optimization_barrier(groups)


def flip_all(arrays):
    return tuple(hop(array, flip=1) for array in arrays)


def gather_logits(place, here, weight):
    prev, cross_here = hop(here, dy=1), cross(here, near=False)
    next_a, next_b = hop(here[:4], dy=-1), hop(here[4:], dy=-1)

    prev, next_a, next_b, cross_here = tie(prev, next_a, next_b, cross_here)
    cross_prev, cross_next_a = cross(prev, near=False), cross(next_a, near=True)
    far_a, far_b = hop(prev[:4], dy=1), hop(next_b, dy=-1)
    here_flip, prev_flip, cross_here_flip = flip_all((here, prev, cross_here))

    cross_prev, cross_next_a, far_a, far_b, here_flip, prev_flip, cross_here_flip = tie(
        cross_prev, cross_next_a, far_a, far_b, here_flip, prev_flip, cross_here_flip
    )
    cross_far_a, cross_far_b = cross(far_a, near=False), cross(far_b, near=False)
    cross_next_b = cross(next_b, near=True)
    own = (prev, here, next_a, next_b, far_a, far_b)
    own_flip = (prev_flip, here_flip) + flip_all(own[2:])
    done = block_logits(place, own, own_flip, weight, 0, None)

    done, rest = tie(done, (cross_prev, cross_next_a, cross_next_b, cross_far_a, cross_far_b))
    rest_flip = flip_all(rest)
    crossed = (rest[0], cross_here) + rest[1:]
    crossed_flip = (rest_flip[0], cross_here_flip) + rest_flip[1:]
    return block_logits(place, crossed, crossed_flip, weight, 1, done)


def coords():
    tok, voc = lax.axis_index("tok"), lax.axis_index("voc")
    return jnp.stack([tok // (2 * NZ), lax.rem(tok // 2, NZ), lax.rem(tok, 2), voc // 2]).astype(jnp.int32)


def token_block(place, column, k):
    x_lo = jnp.where(column == 0, place[0], 1 - place[0])
    return x_lo * NZ + lax.rem(place[1] + NZ - k, NZ)


def to_local(values, place):
    order = jnp.stack([token_block(place, column, k) for column in range(2) for k in range(NZ)])
    return values.reshape(2 * NZ, -1)[order].reshape(-1)


def from_local(values, place):
    order = jnp.stack([token_block(place, x_lo, z) for x_lo in range(2) for z in range(NZ)])
    return values.reshape(2 * NZ, -1)[order].reshape(-1)


PIECES = ((-1, 0), (0, 0), (1, 0), (1, 4), (2, 0), (2, 4))


def logits_kernel(column, place, *refs):
    count = 2 * len(PIECES)
    pieces = refs[:count]
    weight, peak_before, total_before = refs[count : count + 3]
    hidden, logits, peak, total, slots, load_sem, store_sem = refs[-7:]
    rows = pieces[0].shape[1]
    step, steps = pl.program_id(0), pl.num_programs(0)

    @pl.when(step == 0)
    def _():
        for group in range(2):
            for i, piece in enumerate(pieces):
                turn, first = PIECES[i % len(PIECES)]
                if first <= 4 * group < first + piece.shape[0]:
                    core = place[2] if i < len(PIECES) else 1 - place[2]
                    start = core * (rows * NY) + lax.rem(place[3] + turn + NY, NY) * rows
                    to = slots.at[group, :, pl.ds(pl.multiple_of(start, rows), rows)]
                    source = piece.at[pl.ds(4 * group - first, 4)]
                    pltpu.make_async_copy(source, to, load_sem.at[group]).start()
        peak[...] = peak_before[...]
        total[...] = total_before[...]

    def store(group):
        return pltpu.make_async_copy(slots.at[group], hidden.at[2 * column + group], store_sem.at[group])

    pltpu.make_async_copy(slots.at[step], slots.at[step], load_sem.at[step]).wait()
    store(step).start()
    tokens = slots[step].reshape(logits.shape[0], slots.shape[-1])
    values = jnp.dot(tokens, weight[...], preferred_element_type=jnp.float32)
    logits[...] = values
    row_peak = jnp.max(values, axis=1, keepdims=True)
    row_total = jnp.sum(jnp.exp(values - row_peak), axis=1, keepdims=True)
    wide = (values.shape[0], 128)
    for out, stat in ((peak, row_peak), (total, row_total)):
        line = jnp.broadcast_to(stat, wide).T[:1]
        width = out.shape[-1]
        for part in range(4):
            out[token_block(place, column, step * 4 + part)] = line[:, part * width : (part + 1) * width]

    @pl.when(step + 1 == steps)
    def _():
        for group in range(2):
            store(group).wait()


def block_logits(place, mine, others, weight, column, before):
    pieces = [*mine, *others]
    rows, depth = pieces[0].shape[1:]
    width = weight.shape[1]
    block = 2 * NY * rows
    blocks = 2 * NZ
    stat = jax.ShapeDtypeStruct((blocks, 1, block), jnp.float32)
    stat_spec = pl.BlockSpec((blocks, 1, block), lambda step, place: (0, 0, 0))
    any_spec = pl.BlockSpec(memory_space=pl.ANY)
    if before is None:
        extra = [jnp.zeros(stat.shape, stat.dtype)] * 2
        aliases = {}
    else:
        extra = [before[2], before[3], before[0], before[1]]
        aliases = {len(pieces) + 4: 0, len(pieces) + 5: 1}
    return pl.pallas_call(
        functools.partial(logits_kernel, column),
        grid_spec=pltpu.PrefetchScalarGridSpec(
            num_scalar_prefetch=1,
            grid=(2,),
            in_specs=[any_spec] * len(pieces)
            + [pl.BlockSpec((depth, width), lambda *_: (0, 0)), stat_spec, stat_spec]
            + [any_spec] * (len(extra) - 2),
            out_specs=[
                any_spec,
                pl.BlockSpec((4 * block, width), lambda step, place: (2 * column + step, 0)),
                stat_spec,
                stat_spec,
            ],
            scratch_shapes=[
                pltpu.VMEM((2, 4, block, depth), jnp.bfloat16),
                pltpu.SemaphoreType.DMA((2,)),
                pltpu.SemaphoreType.DMA((2,)),
            ],
        ),
        out_shape=[
            jax.ShapeDtypeStruct((4, 4, block, depth), jnp.bfloat16),
            jax.ShapeDtypeStruct((blocks * block, width), jnp.float32),
            stat,
            stat,
        ],
        input_output_aliases=aliases,
        compiler_params=pltpu.CompilerParams(vmem_limit_bytes=56 * 1024 * 1024),
        cost_estimate=pl.CostEstimate(
            flops=blocks * block * depth * width,
            transcendentals=blocks * block * width // 2,
            bytes_accessed=blocks * block * (2 * depth + 2 * width) + 2 * depth * width,
        ),
    )(place, *pieces, weight, *extra)


def rows_kernel(chosen, teacher, aligned, narrow, wide, sem):
    step = pl.program_id(0)
    count = aligned.shape[0]
    parts = sem.shape[0]
    part = narrow.shape[0] // parts

    @pl.when(step == 0)
    def _():
        def load(i):
            span = pl.ds(i * part, part)
            return pltpu.make_async_copy(teacher.at[span], narrow.at[span], sem.at[i])

        for i in range(parts):
            load(i).start()
        for i in range(parts):
            load(i).wait()
            wide[pl.ds(i * part, part), :] = narrow[pl.ds(i * part, part), :].astype(jnp.float32)

    @pl.loop(0, count // 16, unroll=4)
    def _(group):
        first = step * count + group * 16
        picked = [wide[pl.ds(chosen[first + i], 1), :] for i in range(16)]
        rows = jnp.concatenate(picked, axis=0).astype(jnp.bfloat16)
        aligned[pl.ds(pl.multiple_of(group * 16, 16), 16), :] = rows


def take_rows(teacher, chosen):
    rows, width = teacher.shape
    count = rows // 4
    return pl.pallas_call(
        rows_kernel,
        grid_spec=pltpu.PrefetchScalarGridSpec(
            num_scalar_prefetch=1,
            grid=(4,),
            in_specs=[pl.BlockSpec(memory_space=pl.ANY)],
            out_specs=pl.BlockSpec((count, width), lambda step, chosen: (step, 0)),
            scratch_shapes=[
                pltpu.VMEM((rows, width), jnp.bfloat16),
                pltpu.VMEM((rows, width), jnp.float32),
                pltpu.SemaphoreType.DMA((8,)),
            ],
        ),
        out_shape=jax.ShapeDtypeStruct((rows, width), jnp.bfloat16),
        compiler_params=pltpu.CompilerParams(vmem_limit_bytes=56 * 1024 * 1024),
        cost_estimate=pl.CostEstimate(flops=0, transcendentals=0, bytes_accessed=10 * rows * width * 2),
    )(chosen, teacher)


def members(key):
    groups = {}
    for tok in range(2 * NZ * 2):
        for voc in range(NY * 2):
            groups.setdefault(key(tok // (2 * NZ), tok // 2 % NZ, tok % 2, voc), []).append(tok * NY * 2 + voc)
    return list(groups.values())


def from_members(values, groups):
    copies = jnp.broadcast_to(values[None], (len(groups[0]),) + values.shape)
    return lax.all_to_all(copies, AXES, split_axis=0, concat_axis=0, tiled=True, axis_index_groups=groups)


def merge_totals(peaks, totals):
    peak = jnp.max(peaks, axis=0)
    return jnp.stack([peak, jnp.sum(totals * jnp.exp(peaks - peak[None]), axis=0)])


def merge_two(mine, theirs):
    both = jnp.stack([mine, theirs])
    return merge_totals(both[:, 0], both[:, 1])


def merge_over_plane(stats, teacher):
    stats = merge_two(stats, hop(stats, flip=1))
    stats = merge_two(stats, cross(stats, near=True))
    stats = merge_two(stats, hop(stats, dx=2))
    stats = merge_two(stats, turn_pair(stats))
    stats, teacher = tie(stats, teacher)
    return merge_two(stats, hop(stats, dy=2)), teacher


def turn_pair(array):
    pairs = [
        (linear(x, y, z, core), linear(x, y ^ 1, z, core))
        for x in range(NX)
        for y in range(NY)
        for z in range(NZ)
        for core in range(2)
    ]
    return lax.ppermute(array, AXES, pairs)


def make_per_device(tok, voc):
    def per_device(hidden, head_weight, teacher_probs, teacher_row, lengths):
        rows_all = hidden.shape[0] * tok
        here = spread_over_z(hidden)
        by_owner = teacher_probs.reshape(teacher_probs.shape[0], tok, -1).transpose(1, 0, 2)
        here, by_owner = tie(here, by_owner)
        teacher = lax.all_to_all(by_owner, "tok", split_axis=0, concat_axis=0, tiled=True)
        place = coords()
        gathered, logits, local_peak, local_total = gather_logits(place, here, head_weight)
        gathered = gathered.reshape(rows_all, -1)
        along_z = members(lambda x_lo, z, core, voc: (x_lo, core, voc))
        in_plane = members(lambda x_lo, z, core, voc: (z, core))
        stats = jnp.stack([local_peak.reshape(-1), local_total.reshape(-1)])
        stats, teacher = merge_over_plane(stats, teacher)
        aligned = take_rows(teacher.reshape(rows_all, -1), to_local(teacher_row, place))
        aligned = aligned.astype(jnp.float32)
        stats = from_members(stats, along_z)
        row_peak, row_total = merge_totals(stats[:, 0], stats[:, 1])
        row_peak, row_total = to_local(row_peak, place), to_local(row_total, place)
        log_student = logits - row_peak[:, None] - jnp.log(row_total)[:, None]
        student = jnp.exp(log_student)
        log_mix = jnp.log(0.5 * aligned + 0.5 * student)
        grad_prob = 0.5 * (log_student - log_mix)
        local_centre = jnp.sum(student * grad_prob, axis=1)
        centre = from_local(local_centre, place)
        centre = centre + hop(centre, flip=1)
        centre = jnp.sum(from_members(centre, along_z), axis=0)
        centre = to_local(jnp.sum(from_members(centre, in_plane), axis=0), place)
        positions = jnp.arange(SEQ_LEN, dtype=jnp.int32)
        valid_mask = (positions[None, :] < lengths[:, None]).astype(jnp.float32).reshape(-1)
        valid_mask = to_local(valid_mask, place)
        token_count = jnp.sum(lengths).astype(jnp.float32)
        grad_scale = loss_scale / token_count
        dlogits = ((grad_scale * valid_mask)[:, None] * student * (grad_prob - centre[:, None])).astype(
            jnp.bfloat16
        )
        head_grad = lax.dot_general(
            gathered, dlogits, (((0,), (0,)), ((), ())), preferred_element_type=jnp.float32
        )
        return head_grad.astype(jnp.bfloat16)

    return per_device


def solution(mesh):
    return jax.shard_map(
        make_per_device(mesh.shape["tok"], mesh.shape["voc"]),
        mesh=mesh,
        in_specs=(P("tok", None), P(None, ("voc", "tok")), P("tok", "voc"), P(), P()),
        out_specs=P(None, ("voc", "tok")),
        check_vma=False,
    )
```

```python
import functools

import jax
import jax.numpy as jnp
from jax import lax
from jax.experimental import pallas as pl
from jax.experimental.pallas import tpu as pltpu
from jax.sharding import PartitionSpec as P

SEQ_LEN = 128
AXES = ("tok", "voc")

NX, NY, NZ = 4, 4, 8


loss_scale = 1048576.0


def linear(x, y, z, core):
    x, y, z = x % NX, y % NY, z % NZ
    return (((x % 2) * NZ + z) * 2 + core) * (NY * 2) + y * 2 + x // 2


def hop(array, dx=0, dy=0, dz=0, flip=0):
    pairs = [
        (linear(x, y, z, core), linear(x + dx, y + dy, z + dz, core ^ flip))
        for x in range(NX)
        for y in range(NY)
        for z in range(NZ)
        for core in range(2)
    ]
    return lax.ppermute(array, AXES, pairs)


def spread_over_z(hidden):
    rows = hidden.shape[0] // NY
    y = lax.axis_index("voc") // 2
    own = lax.dynamic_slice_in_dim(hidden, y * rows, rows, 0)
    up, down = [own], [own]
    for step in range(1, 4):
        up.append(hop(up[-1], dz=1))
        down.append(hop(down[-1], dz=-1))
    up.append(hop(up[-1], dz=1))
    return jnp.stack([*up, down[3], down[2], down[1]])


def cross(array, near):
    pairs = [
        (linear(x, y, z, core), linear(x + 1 if (x % 2 == 0) == near else x - 1, y, z, core))
        for x in range(NX)
        for y in range(NY)
        for z in range(NZ)
        for core in range(2)
    ]
    return lax.ppermute(array, AXES, pairs)


def tie(*groups):
    return lax.optimization_barrier(groups)


def flip_all(arrays):
    return tuple(hop(array, flip=1) for array in arrays)


def gather_logits(place, here, weight):
    prev, cross_here = hop(here, dy=1), cross(here, near=False)
    next_a, next_b = hop(here[:4], dy=-1), hop(here[4:], dy=-1)

    prev, next_a, next_b, cross_here = tie(prev, next_a, next_b, cross_here)
    cross_prev, cross_next_a = cross(prev, near=False), cross(next_a, near=True)
    far_a, far_b = hop(prev[:4], dy=1), hop(next_b, dy=-1)
    here_flip, prev_flip, cross_here_flip = flip_all((here, prev, cross_here))

    cross_prev, cross_next_a, far_a, far_b, here_flip, prev_flip, cross_here_flip = tie(
        cross_prev, cross_next_a, far_a, far_b, here_flip, prev_flip, cross_here_flip
    )
    cross_far_a, cross_far_b = cross(far_a, near=False), cross(far_b, near=False)
    cross_next_b = cross(next_b, near=True)
    own = (prev, here, next_a, next_b, far_a, far_b)
    own_flip = (prev_flip, here_flip) + flip_all(own[2:])
    done = block_logits(place, own, own_flip, weight, 0, None)

    done, rest = tie(done, (cross_prev, cross_next_a, cross_next_b, cross_far_a, cross_far_b))
    rest_flip = flip_all(rest)
    crossed = (rest[0], cross_here) + rest[1:]
    crossed_flip = (rest_flip[0], cross_here_flip) + rest_flip[1:]
    return block_logits(place, crossed, crossed_flip, weight, 1, done)


def coords():
    tok, voc = lax.axis_index("tok"), lax.axis_index("voc")
    return jnp.stack([tok // (2 * NZ), lax.rem(tok // 2, NZ), lax.rem(tok, 2), voc // 2]).astype(jnp.int32)


def token_block(place, column, k):
    x_lo = jnp.where(column == 0, place[0], 1 - place[0])
    return x_lo * NZ + lax.rem(place[1] + NZ - k, NZ)


def to_local(values, place):
    order = jnp.stack([token_block(place, column, k) for column in range(2) for k in range(NZ)])
    return values.reshape(2 * NZ, -1)[order].reshape(-1)


def from_local(values, place):
    order = jnp.stack([token_block(place, x_lo, z) for x_lo in range(2) for z in range(NZ)])
    return values.reshape(2 * NZ, -1)[order].reshape(-1)


PIECES = ((-1, 0), (0, 0), (1, 0), (1, 4), (2, 0), (2, 4))


def logits_kernel(column, place, *refs):
    count = 2 * len(PIECES)
    pieces = refs[:count]
    weight, peak_before, total_before = refs[count : count + 3]
    hidden, logits, peak, total, slots, load_sem, store_sem = refs[-7:]
    rows = pieces[0].shape[1]
    step, steps = pl.program_id(0), pl.num_programs(0)

    @pl.when(step == 0)
    def _():
        for group in range(2):
            for i, piece in enumerate(pieces):
                turn, first = PIECES[i % len(PIECES)]
                if first <= 4 * group < first + piece.shape[0]:
                    core = place[2] if i < len(PIECES) else 1 - place[2]
                    start = core * (rows * NY) + lax.rem(place[3] + turn + NY, NY) * rows
                    to = slots.at[group, :, pl.ds(pl.multiple_of(start, rows), rows)]
                    source = piece.at[pl.ds(4 * group - first, 4)]
                    pltpu.make_async_copy(source, to, load_sem.at[group]).start()
        peak[...] = peak_before[...]
        total[...] = total_before[...]

    def store(group):
        return pltpu.make_async_copy(slots.at[group], hidden.at[2 * column + group], store_sem.at[group])

    pltpu.make_async_copy(slots.at[step], slots.at[step], load_sem.at[step]).wait()
    store(step).start()
    tokens = slots[step].reshape(logits.shape[0], slots.shape[-1])
    values = jnp.dot(tokens, weight[...], preferred_element_type=jnp.float32)
    logits[...] = values
    row_peak = jnp.max(values, axis=1, keepdims=True)
    row_total = jnp.sum(jnp.exp(values - row_peak), axis=1, keepdims=True)
    wide = (values.shape[0], 128)
    for out, stat in ((peak, row_peak), (total, row_total)):
        line = jnp.broadcast_to(stat, wide).T[:1]
        width = out.shape[-1]
        for part in range(4):
            out[token_block(place, column, step * 4 + part)] = line[:, part * width : (part + 1) * width]

    @pl.when(step + 1 == steps)
    def _():
        for group in range(2):
            store(group).wait()


def block_logits(place, mine, others, weight, column, before):
    pieces = [*mine, *others]
    rows, depth = pieces[0].shape[1:]
    width = weight.shape[1]
    block = 2 * NY * rows
    blocks = 2 * NZ
    stat = jax.ShapeDtypeStruct((blocks, 1, block), jnp.float32)
    stat_spec = pl.BlockSpec((blocks, 1, block), lambda step, place: (0, 0, 0))
    any_spec = pl.BlockSpec(memory_space=pl.ANY)
    if before is None:
        extra = [jnp.zeros(stat.shape, stat.dtype)] * 2
        aliases = {}
    else:
        extra = [before[2], before[3], before[0], before[1]]
        aliases = {len(pieces) + 4: 0, len(pieces) + 5: 1}
    return pl.pallas_call(
        functools.partial(logits_kernel, column),
        grid_spec=pltpu.PrefetchScalarGridSpec(
            num_scalar_prefetch=1,
            grid=(2,),
            in_specs=[any_spec] * len(pieces)
            + [pl.BlockSpec((depth, width), lambda *_: (0, 0)), stat_spec, stat_spec]
            + [any_spec] * (len(extra) - 2),
            out_specs=[
                any_spec,
                pl.BlockSpec((4 * block, width), lambda step, place: (2 * column + step, 0)),
                stat_spec,
                stat_spec,
            ],
            scratch_shapes=[
                pltpu.VMEM((2, 4, block, depth), jnp.bfloat16),
                pltpu.SemaphoreType.DMA((2,)),
                pltpu.SemaphoreType.DMA((2,)),
            ],
        ),
        out_shape=[
            jax.ShapeDtypeStruct((4, 4, block, depth), jnp.bfloat16),
            jax.ShapeDtypeStruct((blocks * block, width), jnp.float32),
            stat,
            stat,
        ],
        input_output_aliases=aliases,
        compiler_params=pltpu.CompilerParams(vmem_limit_bytes=56 * 1024 * 1024),
        cost_estimate=pl.CostEstimate(
            flops=blocks * block * depth * width,
            transcendentals=blocks * block * width // 2,
            bytes_accessed=blocks * block * (2 * depth + 2 * width) + 2 * depth * width,
        ),
    )(place, *pieces, weight, *extra)


def rows_kernel(chosen, teacher, aligned, narrow, wide, sem):
    step = pl.program_id(0)
    count = aligned.shape[0]
    parts = sem.shape[0]
    part = narrow.shape[0] // parts

    @pl.when(step == 0)
    def _():
        def load(i):
            span = pl.ds(i * part, part)
            return pltpu.make_async_copy(teacher.at[span], narrow.at[span], sem.at[i])

        for i in range(parts):
            load(i).start()
        for i in range(parts):
            load(i).wait()
            wide[pl.ds(i * part, part), :] = narrow[pl.ds(i * part, part), :].astype(jnp.float32)

    @pl.loop(0, count // 16, unroll=4)
    def _(group):
        first = step * count + group * 16
        picked = [wide[pl.ds(chosen[first + i], 1), :] for i in range(16)]
        rows = jnp.concatenate(picked, axis=0).astype(jnp.bfloat16)
        aligned[pl.ds(pl.multiple_of(group * 16, 16), 16), :] = rows


def take_rows(teacher, chosen):
    rows, width = teacher.shape
    count = rows // 4
    return pl.pallas_call(
        rows_kernel,
        grid_spec=pltpu.PrefetchScalarGridSpec(
            num_scalar_prefetch=1,
            grid=(4,),
            in_specs=[pl.BlockSpec(memory_space=pl.ANY)],
            out_specs=pl.BlockSpec((count, width), lambda step, chosen: (step, 0)),
            scratch_shapes=[
                pltpu.VMEM((rows, width), jnp.bfloat16),
                pltpu.VMEM((rows, width), jnp.float32),
                pltpu.SemaphoreType.DMA((8,)),
            ],
        ),
        out_shape=jax.ShapeDtypeStruct((rows, width), jnp.bfloat16),
        compiler_params=pltpu.CompilerParams(vmem_limit_bytes=56 * 1024 * 1024),
        cost_estimate=pl.CostEstimate(flops=0, transcendentals=0, bytes_accessed=10 * rows * width * 2),
    )(chosen, teacher)


def members(key):
    groups = {}
    for tok in range(2 * NZ * 2):
        for voc in range(NY * 2):
            groups.setdefault(key(tok // (2 * NZ), tok // 2 % NZ, tok % 2, voc), []).append(tok * NY * 2 + voc)
    return list(groups.values())


def from_members(values, groups):
    copies = jnp.broadcast_to(values[None], (len(groups[0]),) + values.shape)
    return lax.all_to_all(copies, AXES, split_axis=0, concat_axis=0, tiled=True, axis_index_groups=groups)


def peak_and_total(logs):
    peak = jnp.max(logs, axis=0)
    return peak, jnp.sum(jnp.exp(logs - peak[None]), axis=0)


def make_per_device(tok, voc):
    def per_device(hidden, head_weight, teacher_probs, teacher_row, lengths):
        rows_all = hidden.shape[0] * tok
        here = spread_over_z(hidden)
        by_owner = teacher_probs.reshape(teacher_probs.shape[0], tok, -1).transpose(1, 0, 2)
        here, by_owner = tie(here, by_owner)
        teacher = lax.all_to_all(by_owner, "tok", split_axis=0, concat_axis=0, tiled=True)
        place = coords()
        gathered, logits, local_peak, local_total = gather_logits(place, here, head_weight)
        gathered = gathered.reshape(rows_all, -1)
        in_column = members(lambda x_lo, z, core, voc: (x_lo, voc))
        in_plane = members(lambda x_lo, z, core, voc: (z, core))
        log_total = local_peak.reshape(-1) + jnp.log(local_total.reshape(-1))
        log_total, teacher = tie(log_total, teacher)
        aligned = take_rows(teacher.reshape(rows_all, -1), to_local(teacher_row, place))
        log_total = from_members(log_total, in_column)
        log_total, aligned = tie(log_total, aligned)
        aligned = aligned.astype(jnp.float32)
        peak, total = peak_and_total(log_total)
        row_peak, row_total = peak_and_total(from_members(peak + jnp.log(total), in_plane))
        row_peak, row_total = to_local(row_peak, place), to_local(row_total, place)
        log_student = logits - row_peak[:, None] - jnp.log(row_total)[:, None]
        student = jnp.exp(log_student)
        log_mix = jnp.log(0.5 * aligned + 0.5 * student)
        grad_prob = 0.5 * (log_student - log_mix)
        local_centre = jnp.sum(student * grad_prob, axis=1)
        centre = from_local(local_centre, place)
        centre = jnp.sum(from_members(centre, in_column), axis=0)
        centre = to_local(jnp.sum(from_members(centre, in_plane), axis=0), place)
        positions = jnp.arange(SEQ_LEN, dtype=jnp.int32)
        valid_mask = (positions[None, :] < lengths[:, None]).astype(jnp.float32).reshape(-1)
        valid_mask = to_local(valid_mask, place)
        token_count = jnp.sum(lengths).astype(jnp.float32)
        grad_scale = loss_scale / token_count
        dlogits = ((grad_scale * valid_mask)[:, None] * student * (grad_prob - centre[:, None])).astype(
            jnp.bfloat16
        )
        head_grad = lax.dot_general(
            gathered, dlogits, (((0,), (0,)), ((), ())), preferred_element_type=jnp.float32
        )
        return head_grad.astype(jnp.bfloat16)

    return per_device


def solution(mesh):
    return jax.shard_map(
        make_per_device(mesh.shape["tok"], mesh.shape["voc"]),
        mesh=mesh,
        in_specs=(P("tok", None), P(None, ("voc", "tok")), P("tok", "voc"), P(), P()),
        out_specs=P(None, ("voc", "tok")),
        check_vma=False,
    )
```

```python
import functools

import jax
import jax.numpy as jnp
from jax import lax
from jax.experimental import pallas as pl
from jax.experimental.pallas import tpu as pltpu
from jax.sharding import PartitionSpec as P

SEQ_LEN = 128
AXES = ("tok", "voc")

NX, NY, NZ = 4, 4, 8


loss_scale = 1048576.0


def linear(x, y, z, core):
    x, y, z = x % NX, y % NY, z % NZ
    return (((x % 2) * NZ + z) * 2 + core) * (NY * 2) + y * 2 + x // 2


def hop(array, dx=0, dy=0, dz=0, flip=0):
    pairs = [
        (linear(x, y, z, core), linear(x + dx, y + dy, z + dz, core ^ flip))
        for x in range(NX)
        for y in range(NY)
        for z in range(NZ)
        for core in range(2)
    ]
    return lax.ppermute(array, AXES, pairs)


def spread_over_z(hidden):
    rows = hidden.shape[0] // NY
    y = lax.axis_index("voc") // 2
    own = lax.dynamic_slice_in_dim(hidden, y * rows, rows, 0)
    up, down = [own], [own]
    for step in range(1, 4):
        up.append(hop(up[-1], dz=1))
        down.append(hop(down[-1], dz=-1))
    up.append(hop(up[-1], dz=1))
    return jnp.stack([*up, down[3], down[2], down[1]])


def cross(array, near):
    pairs = [
        (linear(x, y, z, core), linear(x + 1 if (x % 2 == 0) == near else x - 1, y, z, core))
        for x in range(NX)
        for y in range(NY)
        for z in range(NZ)
        for core in range(2)
    ]
    return lax.ppermute(array, AXES, pairs)


def tie(*groups):
    return lax.optimization_barrier(groups)


def flip_all(arrays):
    return tuple(hop(array, flip=1) for array in arrays)


def gather_logits(place, here, weight, early):
    prev, cross_here = hop(here, dy=1), cross(here, near=False)
    next_a, next_b = hop(here[:4], dy=-1), hop(here[4:], dy=-1)

    prev, next_a, next_b, cross_here, early = tie(prev, next_a, next_b, cross_here, early)
    cross_prev, cross_next_a = cross(prev, near=False), cross(next_a, near=True)
    far_a, far_b = hop(prev[:4], dy=1), hop(next_b, dy=-1)
    here_flip, prev_flip, cross_here_flip = flip_all((here, prev, cross_here))

    cross_prev, cross_next_a, far_a, far_b, here_flip, prev_flip, cross_here_flip = tie(
        cross_prev, cross_next_a, far_a, far_b, here_flip, prev_flip, cross_here_flip
    )
    cross_far_a, cross_far_b = cross(far_a, near=False), cross(far_b, near=False)
    cross_next_b = cross(next_b, near=True)
    own = (prev, here, next_a, next_b, far_a, far_b)
    own_flip = (prev_flip, here_flip) + flip_all(own[2:])
    done = block_logits(place, own, own_flip, weight, 0, None)

    done, rest = tie(done, (cross_prev, cross_next_a, cross_next_b, cross_far_a, cross_far_b))
    rest_flip = flip_all(rest)
    crossed = (rest[0], cross_here) + rest[1:]
    crossed_flip = (rest_flip[0], cross_here_flip) + rest_flip[1:]
    return block_logits(place, crossed, crossed_flip, weight, 1, done), early


def coords():
    tok, voc = lax.axis_index("tok"), lax.axis_index("voc")
    return jnp.stack([tok // (2 * NZ), lax.rem(tok // 2, NZ), lax.rem(tok, 2), voc // 2]).astype(jnp.int32)


def token_block(place, column, k):
    x_lo = jnp.where(column == 0, place[0], 1 - place[0])
    return x_lo * NZ + lax.rem(place[1] + NZ - k, NZ)


def to_local(values, place):
    order = jnp.stack([token_block(place, column, k) for column in range(2) for k in range(NZ)])
    return values.reshape(2 * NZ, -1)[order].reshape(-1)


def from_local(values, place):
    order = jnp.stack([token_block(place, x_lo, z) for x_lo in range(2) for z in range(NZ)])
    return values.reshape(2 * NZ, -1)[order].reshape(-1)


PIECES = ((-1, 0), (0, 0), (1, 0), (1, 4), (2, 0), (2, 4))


def logits_kernel(column, place, *refs):
    count = 2 * len(PIECES)
    pieces = refs[:count]
    weight, peak_before, total_before = refs[count : count + 3]
    hidden, logits, peak, total, slots, load_sem, store_sem = refs[-7:]
    rows = pieces[0].shape[1]
    step, steps = pl.program_id(0), pl.num_programs(0)

    @pl.when(step == 0)
    def _():
        for group in range(2):
            for i, piece in enumerate(pieces):
                turn, first = PIECES[i % len(PIECES)]
                if first <= 4 * group < first + piece.shape[0]:
                    core = place[2] if i < len(PIECES) else 1 - place[2]
                    start = core * (rows * NY) + lax.rem(place[3] + turn + NY, NY) * rows
                    to = slots.at[group, :, pl.ds(pl.multiple_of(start, rows), rows)]
                    source = piece.at[pl.ds(4 * group - first, 4)]
                    pltpu.make_async_copy(source, to, load_sem.at[group]).start()
        peak[...] = peak_before[...]
        total[...] = total_before[...]

    def store(group):
        return pltpu.make_async_copy(slots.at[group], hidden.at[2 * column + group], store_sem.at[group])

    pltpu.make_async_copy(slots.at[step], slots.at[step], load_sem.at[step]).wait()
    store(step).start()
    tokens = slots[step].reshape(logits.shape[0], slots.shape[-1])
    values = jnp.dot(tokens, weight[...], preferred_element_type=jnp.float32)
    logits[...] = values
    row_peak = jnp.max(values, axis=1, keepdims=True)
    row_total = jnp.sum(jnp.exp(values - row_peak), axis=1, keepdims=True)
    wide = (values.shape[0], 128)
    for out, stat in ((peak, row_peak), (total, row_total)):
        line = jnp.broadcast_to(stat, wide).T[:1]
        width = out.shape[-1]
        for part in range(4):
            out[token_block(place, column, step * 4 + part)] = line[:, part * width : (part + 1) * width]

    @pl.when(step + 1 == steps)
    def _():
        for group in range(2):
            store(group).wait()


def block_logits(place, mine, others, weight, column, before):
    pieces = [*mine, *others]
    rows, depth = pieces[0].shape[1:]
    width = weight.shape[1]
    block = 2 * NY * rows
    blocks = 2 * NZ
    stat = jax.ShapeDtypeStruct((blocks, 1, block), jnp.float32)
    stat_spec = pl.BlockSpec((blocks, 1, block), lambda step, place: (0, 0, 0))
    any_spec = pl.BlockSpec(memory_space=pl.ANY)
    if before is None:
        extra = [jnp.zeros(stat.shape, stat.dtype)] * 2
        aliases = {}
    else:
        extra = [before[2], before[3], before[0], before[1]]
        aliases = {len(pieces) + 4: 0, len(pieces) + 5: 1}
    return pl.pallas_call(
        functools.partial(logits_kernel, column),
        grid_spec=pltpu.PrefetchScalarGridSpec(
            num_scalar_prefetch=1,
            grid=(2,),
            in_specs=[any_spec] * len(pieces)
            + [pl.BlockSpec((depth, width), lambda *_: (0, 0)), stat_spec, stat_spec]
            + [any_spec] * (len(extra) - 2),
            out_specs=[
                any_spec,
                pl.BlockSpec((4 * block, width), lambda step, place: (2 * column + step, 0)),
                stat_spec,
                stat_spec,
            ],
            scratch_shapes=[
                pltpu.VMEM((2, 4, block, depth), jnp.bfloat16),
                pltpu.SemaphoreType.DMA((2,)),
                pltpu.SemaphoreType.DMA((2,)),
            ],
        ),
        out_shape=[
            pltpu.HBM((4, 4, block, depth), jnp.bfloat16),
            pltpu.HBM((blocks * block, width), jnp.float32),
            stat,
            stat,
        ],
        input_output_aliases=aliases,
        compiler_params=pltpu.CompilerParams(vmem_limit_bytes=28 * 1024 * 1024),
        cost_estimate=pl.CostEstimate(
            flops=blocks * block * depth * width,
            transcendentals=blocks * block * width // 2,
            bytes_accessed=blocks * block * (2 * depth + 2 * width) + 2 * depth * width,
        ),
    )(place, *pieces, weight, *extra)


def rows_kernel(chosen, teacher, aligned, narrow, wide, sem):
    step = pl.program_id(0)
    count = aligned.shape[0]
    parts = sem.shape[0]
    part = narrow.shape[0] // parts

    @pl.when(step == 0)
    def _():
        def load(i):
            span = pl.ds(i * part, part)
            return pltpu.make_async_copy(teacher.at[span], narrow.at[span], sem.at[i])

        for i in range(parts):
            load(i).start()
        for i in range(parts):
            load(i).wait()
            wide[pl.ds(i * part, part), :] = narrow[pl.ds(i * part, part), :].astype(jnp.float32)

    @pl.loop(0, count // 16, unroll=4)
    def _(group):
        first = step * count + group * 16
        picked = [wide[pl.ds(chosen[first + i], 1), :] for i in range(16)]
        rows = jnp.concatenate(picked, axis=0).astype(jnp.bfloat16)
        aligned[pl.ds(pl.multiple_of(group * 16, 16), 16), :] = rows


def take_rows(teacher, chosen):
    rows, width = teacher.shape
    count = rows // 4
    return pl.pallas_call(
        rows_kernel,
        grid_spec=pltpu.PrefetchScalarGridSpec(
            num_scalar_prefetch=1,
            grid=(4,),
            in_specs=[pl.BlockSpec(memory_space=pl.ANY)],
            out_specs=pl.BlockSpec((count, width), lambda step, chosen: (step, 0)),
            scratch_shapes=[
                pltpu.VMEM((rows, width), jnp.bfloat16),
                pltpu.VMEM((rows, width), jnp.float32),
                pltpu.SemaphoreType.DMA((8,)),
            ],
        ),
        out_shape=pltpu.HBM((rows, width), jnp.bfloat16),
        compiler_params=pltpu.CompilerParams(vmem_limit_bytes=20 * 1024 * 1024),
        cost_estimate=pl.CostEstimate(flops=0, transcendentals=0, bytes_accessed=10 * rows * width * 2),
    )(chosen, teacher)


def members(key):
    groups = {}
    for tok in range(2 * NZ * 2):
        for voc in range(NY * 2):
            groups.setdefault(key(tok // (2 * NZ), tok // 2 % NZ, tok % 2, voc), []).append(tok * NY * 2 + voc)
    return list(groups.values())


def from_members(values, groups):
    copies = jnp.broadcast_to(values[None], (len(groups[0]),) + values.shape)
    return lax.all_to_all(copies, AXES, split_axis=0, concat_axis=0, tiled=True, axis_index_groups=groups)


def peak_and_total(logs):
    peak = jnp.max(logs, axis=0)
    return peak, jnp.sum(jnp.exp(logs - peak[None]), axis=0)


def make_per_device(tok, voc):
    def per_device(hidden, head_weight, teacher_probs, teacher_row, lengths):
        rows_all = hidden.shape[0] * tok
        here = spread_over_z(hidden)
        by_owner = teacher_probs.reshape(teacher_probs.shape[0], tok, -1).transpose(1, 0, 2)
        place = coords()
        chosen = to_local(teacher_row, place)
        here, by_owner = tie(here, by_owner)
        teacher = lax.all_to_all(by_owner, "tok", split_axis=0, concat_axis=0, tiled=True)
        (gathered, logits, local_peak, local_total), chosen = gather_logits(place, here, head_weight, chosen)
        gathered = gathered.reshape(rows_all, -1)
        in_column = members(lambda x_lo, z, core, voc: (x_lo, voc))
        in_plane = members(lambda x_lo, z, core, voc: (z, core))
        log_total = local_peak.reshape(-1) + jnp.log(local_total.reshape(-1))
        log_total, teacher = tie(log_total, teacher)
        aligned = take_rows(teacher.reshape(rows_all, -1), chosen)
        log_total = from_members(log_total, in_column)
        log_total, aligned = tie(log_total, aligned)
        aligned = aligned.astype(jnp.float32)
        peak, total = peak_and_total(log_total)
        row_peak, row_total = peak_and_total(from_members(peak + jnp.log(total), in_plane))
        row_peak, row_total = to_local(row_peak, place), to_local(row_total, place)
        log_student = logits - row_peak[:, None] - jnp.log(row_total)[:, None]
        student = jnp.exp(log_student)
        grad_prob = 0.5 * (log_student - jnp.log(aligned + student))
        local_centre = jnp.sum(student * grad_prob, axis=1)
        centre = from_local(local_centre, place)
        centre = jnp.sum(from_members(centre, in_column), axis=0)
        centre = to_local(jnp.sum(from_members(centre, in_plane), axis=0), place)
        positions = jnp.arange(SEQ_LEN, dtype=jnp.int32)
        valid_mask = (positions[None, :] < lengths[:, None]).astype(jnp.float32).reshape(-1)
        valid_mask = to_local(valid_mask, place)
        token_count = jnp.sum(lengths).astype(jnp.float32)
        grad_scale = loss_scale / token_count
        dlogits = ((grad_scale * valid_mask)[:, None] * student * (grad_prob - centre[:, None])).astype(
            jnp.bfloat16
        )
        head_grad = lax.dot_general(
            gathered, dlogits, (((0,), (0,)), ((), ())), preferred_element_type=jnp.float32
        )
        return head_grad.astype(jnp.bfloat16)

    return per_device


def solution(mesh):
    return jax.shard_map(
        make_per_device(mesh.shape["tok"], mesh.shape["voc"]),
        mesh=mesh,
        in_specs=(P("tok", None), P(None, ("voc", "tok")), P("tok", "voc"), P(), P()),
        out_specs=P(None, ("voc", "tok")),
        check_vma=False,
    )
```

```python
import functools

import jax
import jax.numpy as jnp
from jax import lax
from jax.experimental import pallas as pl
from jax.experimental.pallas import tpu as pltpu
from jax.sharding import PartitionSpec as P

SEQ_LEN = 128
AXES = ("tok", "voc")

NX, NY, NZ = 4, 4, 8


loss_scale = 1048576.0


def linear(x, y, z, core):
    x, y, z = x % NX, y % NY, z % NZ
    return (((x % 2) * NZ + z) * 2 + core) * (NY * 2) + y * 2 + x // 2


def hop(array, dx=0, dy=0, dz=0, flip=0):
    pairs = [
        (linear(x, y, z, core), linear(x + dx, y + dy, z + dz, core ^ flip))
        for x in range(NX)
        for y in range(NY)
        for z in range(NZ)
        for core in range(2)
    ]
    return lax.ppermute(array, AXES, pairs)


def spread_over_z(hidden):
    rows = hidden.shape[0] // NY
    y = lax.axis_index("voc") // 2
    own = lax.dynamic_slice_in_dim(hidden, y * rows, rows, 0)
    up, down = [own], [own]
    for step in range(1, 4):
        up.append(hop(up[-1], dz=1))
        down.append(hop(down[-1], dz=-1))
    up.append(hop(up[-1], dz=1))
    return jnp.stack([*up, down[3], down[2], down[1]])


def cross(array, near):
    pairs = [
        (linear(x, y, z, core), linear(x + 1 if (x % 2 == 0) == near else x - 1, y, z, core))
        for x in range(NX)
        for y in range(NY)
        for z in range(NZ)
        for core in range(2)
    ]
    return lax.ppermute(array, AXES, pairs)


def tie(*groups):
    return lax.optimization_barrier(groups)


def flip_all(arrays):
    return tuple(hop(array, flip=1) for array in arrays)


def gather_logits(place, here, weight, early):
    prev, cross_here = hop(here, dy=1), cross(here, near=False)
    next_a, next_b = hop(here[:4], dy=-1), hop(here[4:], dy=-1)

    prev, next_a, next_b, cross_here, early = tie(prev, next_a, next_b, cross_here, early)
    cross_prev, cross_next_a = cross(prev, near=False), cross(next_a, near=True)
    far_a, far_b = hop(prev[:4], dy=1), hop(next_b, dy=-1)
    here_flip, prev_flip, cross_here_flip = flip_all((here, prev, cross_here))

    cross_prev, cross_next_a, far_a, far_b, here_flip, prev_flip, cross_here_flip = tie(
        cross_prev, cross_next_a, far_a, far_b, here_flip, prev_flip, cross_here_flip
    )
    cross_far_a, cross_far_b = cross(far_a, near=False), cross(far_b, near=False)
    cross_next_b = cross(next_b, near=True)
    own = (prev, here, next_a, next_b, far_a, far_b)
    own_flip = (prev_flip, here_flip) + flip_all(own[2:])
    done = block_logits(place, own, own_flip, weight, 0, None)

    done, rest = tie(done, (cross_prev, cross_next_a, cross_next_b, cross_far_a, cross_far_b))
    rest_flip = flip_all(rest)
    crossed = (rest[0], cross_here) + rest[1:]
    crossed_flip = (rest_flip[0], cross_here_flip) + rest_flip[1:]
    return block_logits(place, crossed, crossed_flip, weight, 1, done), early


def coords():
    tok, voc = lax.axis_index("tok"), lax.axis_index("voc")
    return jnp.stack([tok // (2 * NZ), lax.rem(tok // 2, NZ), lax.rem(tok, 2), voc // 2]).astype(jnp.int32)


def token_block(place, column, k):
    x_lo = jnp.where(column == 0, place[0], 1 - place[0])
    return x_lo * NZ + lax.rem(place[1] + NZ - k, NZ)


def to_local(values, place):
    order = jnp.stack([token_block(place, column, k) for column in range(2) for k in range(NZ)])
    blocks = values.reshape(*values.shape[:-1], 2 * NZ, -1)
    return jnp.take(blocks, order, axis=-2, mode="clip").reshape(values.shape)


def from_local(values, place):
    order = jnp.stack([token_block(place, x_lo, z) for x_lo in range(2) for z in range(NZ)])
    return values.reshape(2 * NZ, -1)[order].reshape(-1)


PIECES = ((-1, 0), (0, 0), (1, 0), (1, 4), (2, 0), (2, 4))


def logits_kernel(column, place, *refs):
    count = 2 * len(PIECES)
    pieces = refs[:count]
    weight, peak_before, total_before = refs[count : count + 3]
    hidden, logits, peak, total, slots, load_sem, store_sem = refs[-7:]
    rows = pieces[0].shape[1]
    step, steps = pl.program_id(0), pl.num_programs(0)

    @pl.when(step == 0)
    def _():
        for group in range(2):
            for i, piece in enumerate(pieces):
                turn, first = PIECES[i % len(PIECES)]
                if first <= 4 * group < first + piece.shape[0]:
                    core = place[2] if i < len(PIECES) else 1 - place[2]
                    start = core * (rows * NY) + lax.rem(place[3] + turn + NY, NY) * rows
                    to = slots.at[group, :, pl.ds(pl.multiple_of(start, rows), rows)]
                    source = piece.at[pl.ds(4 * group - first, 4)]
                    pltpu.make_async_copy(source, to, load_sem.at[group]).start()
        peak[...] = peak_before[...]
        total[...] = total_before[...]

    def store(group):
        return pltpu.make_async_copy(slots.at[group], hidden.at[2 * column + group], store_sem.at[group])

    pltpu.make_async_copy(slots.at[step], slots.at[step], load_sem.at[step]).wait()
    store(step).start()
    tokens = slots[step].reshape(logits.shape[0], slots.shape[-1])
    values = jnp.dot(tokens, weight[...], preferred_element_type=jnp.float32)
    logits[...] = values
    row_peak = jnp.max(values, axis=1, keepdims=True)
    row_total = jnp.sum(jnp.exp(values - row_peak), axis=1, keepdims=True)
    wide = (values.shape[0], 128)
    for out, stat in ((peak, row_peak), (total, row_total)):
        line = jnp.broadcast_to(stat, wide).T[:1]
        width = out.shape[-1]
        for part in range(4):
            out[token_block(place, column, step * 4 + part)] = line[:, part * width : (part + 1) * width]

    @pl.when(step + 1 == steps)
    def _():
        for group in range(2):
            store(group).wait()


def block_logits(place, mine, others, weight, column, before):
    pieces = [*mine, *others]
    rows, depth = pieces[0].shape[1:]
    width = weight.shape[1]
    block = 2 * NY * rows
    blocks = 2 * NZ
    stat = jax.ShapeDtypeStruct((blocks, 1, block), jnp.float32)
    stat_spec = pl.BlockSpec((blocks, 1, block), lambda step, place: (0, 0, 0))
    any_spec = pl.BlockSpec(memory_space=pl.ANY)
    if before is None:
        extra = [jnp.zeros(stat.shape, stat.dtype)] * 2
        aliases = {}
    else:
        extra = [before[2], before[3], before[0], before[1]]
        aliases = {len(pieces) + 4: 0, len(pieces) + 5: 1}
    return pl.pallas_call(
        functools.partial(logits_kernel, column),
        grid_spec=pltpu.PrefetchScalarGridSpec(
            num_scalar_prefetch=1,
            grid=(2,),
            in_specs=[any_spec] * len(pieces)
            + [pl.BlockSpec((depth, width), lambda *_: (0, 0)), stat_spec, stat_spec]
            + [any_spec] * (len(extra) - 2),
            out_specs=[
                any_spec,
                pl.BlockSpec((4 * block, width), lambda step, place: (2 * column + step, 0)),
                stat_spec,
                stat_spec,
            ],
            scratch_shapes=[
                pltpu.VMEM((2, 4, block, depth), jnp.bfloat16),
                pltpu.SemaphoreType.DMA((2,)),
                pltpu.SemaphoreType.DMA((2,)),
            ],
        ),
        out_shape=[
            pltpu.HBM((4, 4, block, depth), jnp.bfloat16),
            pltpu.HBM((blocks * block, width), jnp.float32),
            stat,
            stat,
        ],
        input_output_aliases=aliases,
        compiler_params=pltpu.CompilerParams(vmem_limit_bytes=28 * 1024 * 1024),
        cost_estimate=pl.CostEstimate(
            flops=blocks * block * depth * width,
            transcendentals=blocks * block * width // 2,
            bytes_accessed=blocks * block * (2 * depth + 2 * width) + 2 * depth * width,
        ),
    )(place, *pieces, weight, *extra)


def rows_kernel(chosen, teacher, aligned, narrow, wide, picked, sem):
    step = pl.program_id(0)
    count, width = aligned.shape
    lines = width // 128
    parts = sem.shape[0]
    part = narrow.shape[0] // parts

    @pl.when(step == 0)
    def _():
        def load(i):
            span = pl.ds(i * part, part)
            return pltpu.make_async_copy(teacher.at[span], narrow.at[span], sem.at[i])

        for i in range(parts):
            load(i).start()
        for i in range(parts):
            load(i).wait()
            for line in range(lines):
                values = narrow[pl.ds(i * part, part), pl.ds(line * 128, 128)].astype(jnp.float32)
                wide[pl.ds(i * part * lines + line, part, stride=lines), :] = values

    @pl.loop(0, count // 16, unroll=4)
    def _(group):
        first = step * count + group * 16
        to = group * 16 * lines
        for i in range(16):
            row = pl.multiple_of(chosen[first + i] * lines, lines)
            picked[pl.ds(pl.multiple_of(to + i * lines, lines), lines), :] = wide[pl.ds(row, lines), :]

    for line in range(lines):
        values = picked[pl.ds(line, count, stride=lines), :]
        aligned[:, pl.ds(line * 128, 128)] = values.astype(jnp.bfloat16)


def take_rows(teacher, chosen):
    rows, width = teacher.shape
    count = rows // 4
    return pl.pallas_call(
        rows_kernel,
        grid_spec=pltpu.PrefetchScalarGridSpec(
            num_scalar_prefetch=1,
            grid=(4,),
            in_specs=[pl.BlockSpec(memory_space=pl.ANY)],
            out_specs=pl.BlockSpec((count, width), lambda step, chosen: (step, 0)),
            scratch_shapes=[
                pltpu.VMEM((rows, width), jnp.bfloat16),
                pltpu.VMEM((rows * (width // 128), 128), jnp.float32),
                pltpu.VMEM((count * (width // 128), 128), jnp.float32),
                pltpu.SemaphoreType.DMA((8,)),
            ],
        ),
        out_shape=pltpu.HBM((rows, width), jnp.bfloat16),
        compiler_params=pltpu.CompilerParams(vmem_limit_bytes=24 * 1024 * 1024),
        cost_estimate=pl.CostEstimate(flops=0, transcendentals=0, bytes_accessed=10 * rows * width * 2),
    )(chosen, teacher)


def members(key):
    groups = {}
    for tok in range(2 * NZ * 2):
        for voc in range(NY * 2):
            groups.setdefault(key(tok // (2 * NZ), tok // 2 % NZ, tok % 2, voc), []).append(tok * NY * 2 + voc)
    return list(groups.values())


def from_members(values, groups):
    copies = jnp.broadcast_to(values[None], (len(groups[0]),) + values.shape)
    return lax.all_to_all(copies, AXES, split_axis=0, concat_axis=0, tiled=True, axis_index_groups=groups)


def peak_and_total(logs):
    peak = jnp.max(logs, axis=0)
    return peak, jnp.sum(jnp.exp(logs - peak[None]), axis=0)


def make_per_device(tok, voc):
    def per_device(hidden, head_weight, teacher_probs, teacher_row, lengths):
        rows_all = hidden.shape[0] * tok
        here = spread_over_z(hidden)
        by_owner = teacher_probs.reshape(teacher_probs.shape[0], tok, -1).transpose(1, 0, 2)
        place = coords()
        chosen = to_local(teacher_row, place)
        here, by_owner = tie(here, by_owner)
        teacher = lax.all_to_all(by_owner, "tok", split_axis=0, concat_axis=0, tiled=True)
        (gathered, logits, local_peak, local_total), chosen = gather_logits(place, here, head_weight, chosen)
        gathered = gathered.reshape(rows_all, -1)
        in_column = members(lambda x_lo, z, core, voc: (x_lo, voc))
        in_plane = members(lambda x_lo, z, core, voc: (z, core))
        log_total = local_peak.reshape(-1) + jnp.log(local_total.reshape(-1))
        log_total, teacher = tie(log_total, teacher)
        aligned = take_rows(teacher.reshape(rows_all, -1), chosen)
        log_total = from_members(log_total, in_column)
        log_total, aligned = tie(log_total, aligned)
        aligned = aligned.astype(jnp.float32)
        peak, total = peak_and_total(log_total)
        row_peak, row_total = peak_and_total(from_members(peak + jnp.log(total), in_plane))
        row_peak, row_total = to_local(jnp.stack([row_peak, row_total]), place)
        log_student = logits - row_peak[:, None] - jnp.log(row_total)[:, None]
        student = jnp.exp(log_student)
        grad_prob = 0.5 * (log_student - jnp.log(aligned + student))
        local_centre = jnp.sum(student * grad_prob, axis=1)
        centre = from_local(local_centre, place)
        centre = jnp.sum(from_members(centre, in_column), axis=0)
        centre = to_local(jnp.sum(from_members(centre, in_plane), axis=0), place)
        positions = jnp.arange(SEQ_LEN, dtype=jnp.int32)
        valid_mask = (positions[None, :] < lengths[:, None]).astype(jnp.float32).reshape(-1)
        valid_mask = to_local(valid_mask, place)
        token_count = jnp.sum(lengths).astype(jnp.float32)
        grad_scale = loss_scale / token_count
        dlogits = ((grad_scale * valid_mask)[:, None] * student * (grad_prob - centre[:, None])).astype(
            jnp.bfloat16
        )
        head_grad = lax.dot_general(
            gathered, dlogits, (((0,), (0,)), ((), ())), preferred_element_type=jnp.float32
        )
        return head_grad.astype(jnp.bfloat16)

    return per_device


def solution(mesh):
    return jax.shard_map(
        make_per_device(mesh.shape["tok"], mesh.shape["voc"]),
        mesh=mesh,
        in_specs=(P("tok", None), P(None, ("voc", "tok")), P("tok", "voc"), P(), P()),
        out_specs=P(None, ("voc", "tok")),
        check_vma=False,
    )
```

```python
import functools

import jax
import jax.numpy as jnp
from jax import lax
from jax.experimental import pallas as pl
from jax.experimental.pallas import tpu as pltpu
from jax.sharding import PartitionSpec as P

SEQ_LEN = 128
AXES = ("tok", "voc")

NX, NY, NZ = 4, 4, 8


loss_scale = 1048576.0


def linear(x, y, z, core):
    x, y, z = x % NX, y % NY, z % NZ
    return (((x % 2) * NZ + z) * 2 + core) * (NY * 2) + y * 2 + x // 2


def hop(array, dx=0, dy=0, dz=0, flip=0):
    pairs = [
        (linear(x, y, z, core), linear(x + dx, y + dy, z + dz, core ^ flip))
        for x in range(NX)
        for y in range(NY)
        for z in range(NZ)
        for core in range(2)
    ]
    return lax.ppermute(array, AXES, pairs)


def spread_over_z(hidden):
    rows = hidden.shape[0] // NY
    y = lax.axis_index("voc") // 2
    own = lax.dynamic_slice_in_dim(hidden, y * rows, rows, 0)
    up, down = [own], [own]
    for step in range(1, 4):
        up.append(hop(up[-1], dz=1))
        down.append(hop(down[-1], dz=-1))
    half = rows // 2
    opposite = jnp.concatenate([hop(up[2][:half], dz=2), hop(down[2][half:], dz=-2)])
    return jnp.stack([*up, opposite, down[3], down[2], down[1]])


def cross(array, near):
    pairs = [
        (linear(x, y, z, core), linear(x + 1 if (x % 2 == 0) == near else x - 1, y, z, core))
        for x in range(NX)
        for y in range(NY)
        for z in range(NZ)
        for core in range(2)
    ]
    return lax.ppermute(array, AXES, pairs)


def tie(*groups):
    return lax.optimization_barrier(groups)


def flip_all(arrays):
    return tuple(hop(array, flip=1) for array in arrays)


def gather_logits(place, here, weight, early):
    prev, cross_here = hop(here, dy=1), cross(here, near=False)
    next_a, next_b = hop(here[:4], dy=-1), hop(here[4:], dy=-1)

    prev, next_a, next_b, cross_here, early = tie(prev, next_a, next_b, cross_here, early)
    cross_prev, cross_next_a = cross(prev, near=False), cross(next_a, near=True)
    far_a, far_b = hop(prev[:4], dy=1), hop(next_b, dy=-1)
    here_flip, prev_flip, cross_here_flip = flip_all((here, prev, cross_here))

    cross_prev, cross_next_a, far_a, far_b, here_flip, prev_flip, cross_here_flip = tie(
        cross_prev, cross_next_a, far_a, far_b, here_flip, prev_flip, cross_here_flip
    )
    cross_far_a, cross_far_b = cross(far_a, near=False), cross(far_b, near=False)
    cross_next_b = cross(next_b, near=True)
    own = (prev, here, next_a, next_b, far_a, far_b)
    own_flip = (prev_flip, here_flip) + flip_all(own[2:])
    done = block_logits(place, own, own_flip, weight, 0, None)

    done, rest = tie(done, (cross_prev, cross_next_a, cross_next_b, cross_far_a, cross_far_b))
    rest_flip = flip_all(rest)
    crossed = (rest[0], cross_here) + rest[1:]
    crossed_flip = (rest_flip[0], cross_here_flip) + rest_flip[1:]
    return block_logits(place, crossed, crossed_flip, weight, 1, done), early


def coords():
    tok, voc = lax.axis_index("tok"), lax.axis_index("voc")
    return jnp.stack([tok // (2 * NZ), lax.rem(tok // 2, NZ), lax.rem(tok, 2), voc // 2]).astype(jnp.int32)


def token_block(place, column, k):
    x_lo = jnp.where(column == 0, place[0], 1 - place[0])
    return x_lo * NZ + lax.rem(place[1] + NZ - k, NZ)


def to_local(values, place):
    order = jnp.stack([token_block(place, column, k) for column in range(2) for k in range(NZ)])
    blocks = values.reshape(*values.shape[:-1], 2 * NZ, -1)
    return jnp.take(blocks, order, axis=-2, mode="clip").reshape(values.shape)


def from_local(values, place):
    order = jnp.stack([token_block(place, x_lo, z) for x_lo in range(2) for z in range(NZ)])
    return values.reshape(2 * NZ, -1)[order].reshape(-1)


PIECES = ((-1, 0), (0, 0), (1, 0), (1, 4), (2, 0), (2, 4))


def logits_kernel(column, place, *refs):
    count = 2 * len(PIECES)
    pieces = refs[:count]
    weight, peak_before, total_before = refs[count : count + 3]
    hidden, logits, peak, total, slots, load_sem, store_sem = refs[-7:]
    rows = pieces[0].shape[1]
    step, steps = pl.program_id(0), pl.num_programs(0)

    @pl.when(step == 0)
    def _():
        for group in range(2):
            for i, piece in enumerate(pieces):
                turn, first = PIECES[i % len(PIECES)]
                if first <= 4 * group < first + piece.shape[0]:
                    core = place[2] if i < len(PIECES) else 1 - place[2]
                    start = core * (rows * NY) + lax.rem(place[3] + turn + NY, NY) * rows
                    to = slots.at[group, :, pl.ds(pl.multiple_of(start, rows), rows)]
                    source = piece.at[pl.ds(4 * group - first, 4)]
                    pltpu.make_async_copy(source, to, load_sem.at[group]).start()
        peak[...] = peak_before[...]
        total[...] = total_before[...]

    def store(group):
        return pltpu.make_async_copy(slots.at[group], hidden.at[2 * column + group], store_sem.at[group])

    pltpu.make_async_copy(slots.at[step], slots.at[step], load_sem.at[step]).wait()
    store(step).start()
    tokens = slots[step].reshape(logits.shape[0], slots.shape[-1])
    values = jnp.dot(tokens, weight[...], preferred_element_type=jnp.float32)
    logits[...] = values
    row_peak = jnp.max(values, axis=1, keepdims=True)
    row_total = jnp.sum(jnp.exp(values - row_peak), axis=1, keepdims=True)
    wide = (values.shape[0], 128)
    for out, stat in ((peak, row_peak), (total, row_total)):
        line = jnp.broadcast_to(stat, wide).T[:1]
        width = out.shape[-1]
        for part in range(4):
            out[token_block(place, column, step * 4 + part)] = line[:, part * width : (part + 1) * width]

    @pl.when(step + 1 == steps)
    def _():
        for group in range(2):
            store(group).wait()


def block_logits(place, mine, others, weight, column, before):
    pieces = [*mine, *others]
    rows, depth = pieces[0].shape[1:]
    width = weight.shape[1]
    block = 2 * NY * rows
    blocks = 2 * NZ
    stat = jax.ShapeDtypeStruct((blocks, 1, block), jnp.float32)
    stat_spec = pl.BlockSpec((blocks, 1, block), lambda step, place: (0, 0, 0))
    any_spec = pl.BlockSpec(memory_space=pl.ANY)
    if before is None:
        extra = [jnp.zeros(stat.shape, stat.dtype)] * 2
        aliases = {}
    else:
        extra = [before[2], before[3], before[0], before[1]]
        aliases = {len(pieces) + 4: 0, len(pieces) + 5: 1}
    return pl.pallas_call(
        functools.partial(logits_kernel, column),
        grid_spec=pltpu.PrefetchScalarGridSpec(
            num_scalar_prefetch=1,
            grid=(2,),
            in_specs=[any_spec] * len(pieces)
            + [pl.BlockSpec((depth, width), lambda *_: (0, 0)), stat_spec, stat_spec]
            + [any_spec] * (len(extra) - 2),
            out_specs=[
                any_spec,
                pl.BlockSpec((4 * block, width), lambda step, place: (2 * column + step, 0)),
                stat_spec,
                stat_spec,
            ],
            scratch_shapes=[
                pltpu.VMEM((2, 4, block, depth), jnp.bfloat16),
                pltpu.SemaphoreType.DMA((2,)),
                pltpu.SemaphoreType.DMA((2,)),
            ],
        ),
        out_shape=[
            pltpu.HBM((4, 4, block, depth), jnp.bfloat16),
            pltpu.HBM((blocks * block, width), jnp.float32),
            stat,
            stat,
        ],
        input_output_aliases=aliases,
        compiler_params=pltpu.CompilerParams(vmem_limit_bytes=28 * 1024 * 1024),
        cost_estimate=pl.CostEstimate(
            flops=blocks * block * depth * width,
            transcendentals=blocks * block * width // 2,
            bytes_accessed=blocks * block * (2 * depth + 2 * width) + 2 * depth * width,
        ),
    )(place, *pieces, weight, *extra)


def rows_kernel(chosen, teacher, aligned, narrow, wide, picked, sem):
    step = pl.program_id(0)
    count, width = aligned.shape
    lines = width // 128
    parts = sem.shape[0]
    part = narrow.shape[0] // parts

    @pl.when(step == 0)
    def _():
        def load(i):
            span = pl.ds(i * part, part)
            return pltpu.make_async_copy(teacher.at[span], narrow.at[span], sem.at[i])

        for i in range(parts):
            load(i).start()
        for i in range(parts):
            load(i).wait()
            for line in range(lines):
                values = narrow[pl.ds(i * part, part), pl.ds(line * 128, 128)].astype(jnp.float32)
                wide[pl.ds(i * part * lines + line, part, stride=lines), :] = values

    @pl.loop(0, count // 16, unroll=4)
    def _(group):
        first = step * count + group * 16
        to = group * 16 * lines
        for i in range(16):
            row = pl.multiple_of(chosen[first + i] * lines, lines)
            picked[pl.ds(pl.multiple_of(to + i * lines, lines), lines), :] = wide[pl.ds(row, lines), :]

    for line in range(lines):
        values = picked[pl.ds(line, count, stride=lines), :]
        aligned[:, pl.ds(line * 128, 128)] = values.astype(jnp.bfloat16)


def take_rows(teacher, chosen):
    rows, width = teacher.shape
    count = rows // 4
    return pl.pallas_call(
        rows_kernel,
        grid_spec=pltpu.PrefetchScalarGridSpec(
            num_scalar_prefetch=1,
            grid=(4,),
            in_specs=[pl.BlockSpec(memory_space=pl.ANY)],
            out_specs=pl.BlockSpec((count, width), lambda step, chosen: (step, 0)),
            scratch_shapes=[
                pltpu.VMEM((rows, width), jnp.bfloat16),
                pltpu.VMEM((rows * (width // 128), 128), jnp.float32),
                pltpu.VMEM((count * (width // 128), 128), jnp.float32),
                pltpu.SemaphoreType.DMA((8,)),
            ],
        ),
        out_shape=pltpu.HBM((rows, width), jnp.bfloat16),
        compiler_params=pltpu.CompilerParams(vmem_limit_bytes=24 * 1024 * 1024),
        cost_estimate=pl.CostEstimate(flops=0, transcendentals=0, bytes_accessed=10 * rows * width * 2),
    )(chosen, teacher)


def members(key):
    groups = {}
    for tok in range(2 * NZ * 2):
        for voc in range(NY * 2):
            groups.setdefault(key(tok // (2 * NZ), tok // 2 % NZ, tok % 2, voc), []).append(tok * NY * 2 + voc)
    return list(groups.values())


def from_members(values, groups):
    copies = jnp.broadcast_to(values[None], (len(groups[0]),) + values.shape)
    return lax.all_to_all(copies, AXES, split_axis=0, concat_axis=0, tiled=True, axis_index_groups=groups)


def peak_and_total(logs):
    peak = jnp.max(logs, axis=0)
    return peak, jnp.sum(jnp.exp(logs - peak[None]), axis=0)


def make_per_device(tok, voc):
    def per_device(hidden, head_weight, teacher_probs, teacher_row, lengths):
        rows_all = hidden.shape[0] * tok
        here = spread_over_z(hidden)
        by_owner = teacher_probs.reshape(teacher_probs.shape[0], tok, -1).transpose(1, 0, 2)
        place = coords()
        chosen = to_local(teacher_row, place)
        here, by_owner = tie(here, by_owner)
        teacher = lax.all_to_all(by_owner, "tok", split_axis=0, concat_axis=0, tiled=True)
        (gathered, logits, local_peak, local_total), chosen = gather_logits(place, here, head_weight, chosen)
        gathered = gathered.reshape(rows_all, -1)
        in_column = members(lambda x_lo, z, core, voc: (x_lo, voc))
        in_plane = members(lambda x_lo, z, core, voc: (z, core))
        log_total = local_peak.reshape(-1) + jnp.log(local_total.reshape(-1))
        log_total, teacher = tie(log_total, teacher)
        aligned = take_rows(teacher.reshape(rows_all, -1), chosen)
        log_total = from_members(log_total, in_column)
        log_total, aligned = tie(log_total, aligned)
        aligned = aligned.astype(jnp.float32)
        peak, total = peak_and_total(log_total)
        row_peak, row_total = peak_and_total(from_members(peak + jnp.log(total), in_plane))
        row_peak, row_total = to_local(jnp.stack([row_peak, row_total]), place)
        log_student = logits - row_peak[:, None] - jnp.log(row_total)[:, None]
        student = jnp.exp(log_student)
        grad_prob = 0.5 * (log_student - jnp.log(aligned + student))
        local_centre = jnp.sum(student * grad_prob, axis=1)
        centre = from_local(local_centre, place)
        centre = jnp.sum(from_members(centre, in_column), axis=0)
        centre = to_local(jnp.sum(from_members(centre, in_plane), axis=0), place)
        positions = jnp.arange(SEQ_LEN, dtype=jnp.int32)
        valid_mask = (positions[None, :] < lengths[:, None]).astype(jnp.float32).reshape(-1)
        valid_mask = to_local(valid_mask, place)
        token_count = jnp.sum(lengths).astype(jnp.float32)
        grad_scale = loss_scale / token_count
        dlogits = ((grad_scale * valid_mask)[:, None] * student * (grad_prob - centre[:, None])).astype(
            jnp.bfloat16
        )
        head_grad = lax.dot_general(
            gathered, dlogits, (((0,), (0,)), ((), ())), preferred_element_type=jnp.float32
        )
        return head_grad.astype(jnp.bfloat16)

    return per_device


def solution(mesh):
    return jax.shard_map(
        make_per_device(mesh.shape["tok"], mesh.shape["voc"]),
        mesh=mesh,
        in_specs=(P("tok", None), P(None, ("voc", "tok")), P("tok", "voc"), P(), P()),
        out_specs=P(None, ("voc", "tok")),
        check_vma=False,
    )
```
